32 devices in a mesh: section: 2 (over x), lat: 4 (over y, core), lon: 4 (over z).
Axes of the slice: x: 2, y: 2, z: 4, core: 2. Of those that a mesh axis runs over, the one named last changes fastest.
Arguments:
- start: bfloat16 [2, 12, 32, 1024], P('section', None, 'lat', 'lon'), may hold values from -6 to 6
- prior_mean: bfloat16 [12, 32, 1024], P(None, 'lat', 'lon'), may hold values from -6 to 6
- lift_w: bfloat16 [2, 24, 128], P('section'), may hold values from -1.25 to 1.25
- noise_gain: float32 [2, 128], P('section'), may hold values from -8 to 8
- conv0a: bfloat16 [2, 9, 128, 128], P('section'), may hold values from -0.25 to 0.25
- expand: bfloat16 [2, 128, 256], P('section'), may hold values from -0.5 to 0.5
- conv1a: bfloat16 [2, 9, 256, 256], P('section'), may hold values from -0.1875 to 0.1875
- conv1b: bfloat16 [2, 9, 256, 256], P('section'), may hold values from -0.1875 to 0.1875
- shrink: bfloat16 [2, 256, 128], P('section'), may hold values from -0.375 to 0.375
- conv0b: bfloat16 [2, 9, 128, 128], P('section'), may hold values from -0.25 to 0.25
- head: bfloat16 [2, 128, 12], P('section'), may hold values from -0.5 to 0.5
Outputs:
- results: bfloat16 [2, 12, 32, 1024], P('section', None, 'lat', 'lon')
The draws below stay inside these ranges and needn't reach their ends.
All inputs are finite; a program needn't handle non-finite values.
Results may differ from the reference program's by a relative error of at most 0.013.
Values may be sent and summed in bfloat16 or wider, within the bound.
A program may use at most 64 MiB of HBM per device.

```python
import math
import jax
import jax.numpy as jnp
from jax import lax

VARS = 12
C0 = 128
C1 = 256
HEIGHT = 32
WIDTH = 1024


def level_of(stream_key, shape, split, low, top_value):
    loudness = 1.0
    for position, parts in split:
        heights = jax.random.uniform(jax.random.fold_in(jax.random.fold_in(stream_key, 6), position), (parts,), jnp.float32, low / len(split), top_value / len(split))
        loudness = loudness * jnp.repeat(jnp.exp(heights), shape[position] // parts).reshape((-1,) + (1,) * (len(shape) - 1 - position))
    return loudness


def noise(key, shape, deviation, reach, split=(), dtype=jnp.bfloat16):
    array = jax.random.normal(key, shape, jnp.float32) * deviation
    if len(split) > 0:
        array = level_of(key, shape, split, -0.22, 0.18) * array
    return jnp.clip(array, min=-reach, max=reach).astype(dtype)


def setup_inputs(seed: int = 0) -> dict:
    splits = jax.random.split(jax.random.key(seed), 12)
    return {
        "start": noise(splits[0], (2, VARS, HEIGHT, WIDTH), 1.0, 6.0, ((0, 2), (2, 4), (3, 4))),
        "prior_mean": noise(splits[1], (VARS, HEIGHT, WIDTH), 1.0, 6.0, ((1, 4), (2, 4))),
        "lift_w": noise(splits[2], (2, 2 * VARS, C0), (2 * VARS) ** -0.5, 1.25, ((0, 2),)),
        "noise_gain": noise(splits[3], (2, C0), 2.0, 8.0, ((0, 2),), jnp.float32),
        "conv0a": noise(splits[4], (2, 9, C0, C0), (4 * C0) ** -0.5, 0.25, ((0, 2),)),
        "expand": noise(splits[5], (2, C0, C1), C0 ** -0.5, 0.5, ((0, 2),)),
        "conv1a": noise(splits[6], (2, 9, C1, C1), (4 * C1) ** -0.5, 0.1875, ((0, 2),)),
        "conv1b": noise(splits[7], (2, 9, C1, C1), (4 * C1) ** -0.5, 0.1875, ((0, 2),)),
        "shrink": noise(splits[8], (2, C1, C0), C1 ** -0.5, 0.375, ((0, 2),)),
        "conv0b": noise(splits[9], (2, 9, C0, C0), (4 * C0) ** -0.5, 0.25, ((0, 2),)),
        "head": noise(splits[10], (2, C0, VARS), C0 ** -0.5, 0.5, ((0, 2),)),
    }


sigma_data = 0.5
sigma_high = 2.0
sigma_low = 0.5

def precondition(sigma):
    total = sigma * sigma + sigma_data * sigma_data
    return (1.0 / math.sqrt(total), sigma_data * sigma_data / total, sigma * sigma_data / math.sqrt(total), math.log(sigma) / 4.0)

def pad_grid(field):
    wrapped = jnp.concatenate([field[:, -1:], field, field[:, :1]], axis=1)
    return jnp.pad(wrapped, ((1, 1), (0, 0), (0, 0)))

def convolve(padded, kernel, height, breadth):
    channels = padded.shape[-1]
    total = jnp.zeros((height * breadth, kernel.shape[-1]), jnp.float32)
    for offset in range(9):
        down, across = divmod(offset, 3)
        window = padded[down:down + height, across:across + breadth].reshape(height * breadth, channels)
        total = total + jnp.dot(window, kernel[offset], preferred_element_type=jnp.float32)
    return total.reshape(height, breadth, -1)

def network(state, prior, shift, weights):
    lift_w, conv0a, expand, conv1a, conv1b, shrink, conv0b, head = weights
    fields = jnp.concatenate([state, prior], axis=0)
    channels, height, breadth = fields.shape
    flat = fields.reshape(channels, height * breadth)
    hidden = lax.dot_general(flat, lift_w, (((0,), (0,)), ((), ())), preferred_element_type=jnp.float32)
    lifted = jax.nn.silu(hidden + shift).astype(jnp.bfloat16).reshape(height, breadth, -1)
    first_level = jax.nn.silu(convolve(pad_grid(lifted), conv0a, height, breadth)).astype(jnp.bfloat16)
    half_h = height // 2
    half_b = breadth // 2
    pooled = (lax.optimization_barrier(jnp.sum(first_level.reshape(half_h, 2, half_b, 2, -1).astype(jnp.float32), axis=(1, 3))) * 0.25).astype(jnp.bfloat16)
    widened = jnp.dot(pooled.reshape(half_h * half_b, -1), expand, preferred_element_type=jnp.float32).astype(jnp.bfloat16).reshape(half_h, half_b, -1)
    inner = jax.nn.silu(convolve(pad_grid(widened), conv1a, half_h, half_b)).astype(jnp.bfloat16)
    coarse_out = (jax.nn.silu(convolve(pad_grid(inner), conv1b, half_h, half_b)) + widened.astype(jnp.float32)).astype(jnp.bfloat16)
    projected = jnp.dot(coarse_out.reshape(half_h * half_b, -1), shrink, preferred_element_type=jnp.float32).reshape(half_h, 1, half_b, 1, -1)
    spread = jnp.broadcast_to(projected, (half_h, 2, half_b, 2, projected.shape[-1])).reshape(height, breadth, -1)
    merged = (spread + first_level.astype(jnp.float32)).astype(jnp.bfloat16)
    last_level = jax.nn.silu(convolve(pad_grid(merged), conv0b, height, breadth)).astype(jnp.bfloat16)
    output = lax.dot_general(head, last_level.reshape(height * breadth, -1), (((0,), (1,)), ((), ())), preferred_element_type=jnp.float32)
    return output.reshape(-1, height, breadth)

def reference(start, prior_mean, lift_w, noise_gain, conv0a, expand, conv1a, conv1b, shrink, conv0b, head):

    def weights_of(section):
        return (lift_w[section], conv0a[section], expand[section], conv1a[section], conv1b[section], shrink[section], conv0b[section], head[section])
    high = precondition(sigma_high)
    low = precondition(sigma_low)
    zero_shift = jnp.zeros((lift_w.shape[-1],), jnp.float32)
    mean_next = network(start[0], prior_mean, zero_shift, weights_of(0)).astype(jnp.bfloat16)
    noisy = sigma_high * start[1].astype(jnp.float32)
    first_input = (high[0] * noisy).astype(jnp.bfloat16)
    first_out = network(first_input, prior_mean, high[3] * noise_gain[1], weights_of(1))
    first_denoised = high[1] * noisy + high[2] * first_out
    moved = noisy + (sigma_low - sigma_high) / sigma_high * (noisy - first_denoised)
    second_input = (low[0] * moved).astype(jnp.bfloat16)
    second_out = network(second_input, prior_mean, low[3] * noise_gain[1], weights_of(1))
    second_denoised = low[1] * moved + low[2] * second_out
    sample = (prior_mean.astype(jnp.float32) + second_denoised).astype(jnp.bfloat16)
    return jnp.stack([sample, mean_next])
```

```python
import functools
import math

import jax
import jax.numpy as jnp
from jax import lax
from jax.experimental import pallas as pl
from jax.experimental.pallas import tpu as pltpu
from jax.sharding import PartitionSpec as P

sigma_data = 0.5
sigma_high = 2.0
sigma_low = 0.5

MESH = pl.DeviceIdType.MESH
bf16 = jnp.bfloat16
f32 = jnp.float32

HALO = 8
MESSAGES = ((0, 1), (0, -1), (1, 1), (1, -1), (-1, 1), (-1, -1), (1, 0), (-1, 0))


def precondition(sigma):
    total = sigma * sigma + sigma_data * sigma_data
    return (
        1.0 / math.sqrt(total),
        sigma_data * sigma_data / total,
        sigma * sigma_data / math.sqrt(total),
        math.log(sigma) / 4.0,
    )


def silu(x):
    half = 0.5 * x
    return half + half * jnp.tanh(half)


def dot(a, b):
    return jnp.dot(a, b, preferred_element_type=f32)


def dot_nt(a, b):
    return lax.dot_general(a, b, (((1,), (1,)), ((), ())), preferred_element_type=f32)


def kernel(
    n_lat,
    n_lon,
    start,
    prior,
    lift_w,
    gain,
    conv0a,
    expand,
    conv1a,
    conv1b,
    shrink,
    conv0b,
    head,
    out,
    w0a,
    w0b,
    w1a,
    w1b,
    wlift,
    whead,
    mine,
    edges1,
    lat1,
    rim1,
    state2,
    edges2,
    lat2,
    rim2,
    given_t,
    moved,
    shift,
    cells,
    lifted,
    first,
    widened,
    inner,
    merged,
    last,
    finished,
    arrived,
    wsem,
    ssem,
    rsem,
    swap_s,
    swap_r,
):
    section = lax.axis_index("section")
    lat = lax.axis_index("lat")
    lon = lax.axis_index("lon")
    diffuse = section == 1
    variables, rows, cols = start.shape[1:]
    c0 = lift_w.shape[-1]
    half = cols // 2
    wide = half + 2 * HALO
    pairs = rows // 2
    used = variables * rows
    lanes = given_t.shape[1]
    high = precondition(sigma_high)
    low = precondition(sigma_low)

    def target(dlat, dlon):
        return (section, lat + dlat, lax.rem(lon + dlon + n_lon, n_lon))

    def present(dlat):
        if dlat < 0:
            return lat > 0
        return lat < n_lat - 1

    def guarded(dlat, action):
        if dlat == 0:
            action()
        else:
            pl.when(present(dlat))(action)

    partner = (1 - section, lat, lon)

    barrier = pltpu.get_barrier_semaphore()
    pl.semaphore_signal(barrier, inc=1, device_id=partner, device_id_type=MESH)
    for dlat, dlon in MESSAGES:
        guarded(
            dlat,
            functools.partial(
                pl.semaphore_signal,
                barrier,
                inc=1,
                device_id=target(dlat, dlon),
                device_id_type=MESH,
            ),
        )

    copies = [
        pltpu.make_async_copy(
            conv0a.at[0], w0a.at[pl.ds(0, 3), :, :, pl.ds(0, c0)], wsem.at[0]
        ),
        pltpu.make_async_copy(
            conv0a.at[0], w0a.at[pl.ds(1, 3), :, :, pl.ds(c0, c0)], wsem.at[1]
        ),
        pltpu.make_async_copy(conv1a.at[0], w1a, wsem.at[2]),
        pltpu.make_async_copy(conv1b.at[0], w1b, wsem.at[3]),
        pltpu.make_async_copy(
            conv0b.at[0], w0b.at[pl.ds(0, 3), :, :, pl.ds(0, c0)], wsem.at[4]
        ),
        pltpu.make_async_copy(
            conv0b.at[0], w0b.at[pl.ds(1, 3), :, :, pl.ds(c0, c0)], wsem.at[5]
        ),
    ]
    for copy in copies:
        copy.start()
    for folded in (w0a, w0b):
        blank = jnp.zeros((3, c0, c0), bf16)
        folded[3, :, :, 0:c0] = blank
        folded[0, :, :, c0 : 2 * c0] = blank

    i = lax.broadcasted_iota(jnp.int32, (cols, cols), 0)
    j = lax.broadcasted_iota(jnp.int32, (cols, cols), 1)
    order = jnp.where(
        j == jnp.where(i < half, 2 * i, 2 * (i - half) + 1), 1.0, 0.0
    ).astype(bf16)

    def turned(x):
        flat = x.reshape(used, cols)
        if lanes > used:
            flat = jnp.concatenate([flat, jnp.zeros((lanes - used, cols), f32)], axis=0)
        return dot_nt(order, flat.astype(bf16))

    def straight(y):
        a = lax.broadcasted_iota(jnp.int32, (lanes, lanes), 0)
        b = lax.broadcasted_iota(jnp.int32, (lanes, lanes), 1)
        eye = jnp.where(a == b, 1.0, 0.0).astype(bf16)
        return dot(dot_nt(eye, y).astype(bf16), order)[:used]

    def borders(t, edges):
        edges[0] = jnp.concatenate([t[half - HALO : half], t[cols - HALO : cols]], axis=0).astype(bf16)
        edges[1] = jnp.concatenate([t[0:HALO], t[half : half + HALO]], axis=0).astype(bf16)

    given = start[0].astype(f32)
    scale = jnp.where(diffuse, high[0] * sigma_high, 1.0).astype(f32)
    state = turned(scale * given)
    prior_t = turned(prior[...].astype(f32))
    given_t[...] = turned(given)
    full = jnp.concatenate([state, prior_t], axis=1)
    mine[...] = full.astype(bf16)
    borders(full, edges1)

    pl.semaphore_wait(
        barrier,
        3 + jnp.where(lat > 0, 3, 0) + jnp.where(lat < n_lat - 1, 3, 0),
    )

    def message(step, index, block, edges, lat_in, rim_in):
        dlat, dlon = MESSAGES[index]
        if dlon == 0:
            source, landing = block, lat_in.at[0 if dlat > 0 else 1]
        else:
            side = 0 if dlon > 0 else 1
            source, landing = edges.at[side], rim_in.at[side, 1 - dlat]
        return pltpu.make_async_remote_copy(
            src_ref=source,
            dst_ref=landing,
            send_sem=ssem.at[step, index],
            recv_sem=rsem.at[step, index],
            device_id=target(dlat, dlon),
            device_id_type=MESH,
        )

    exchanges = (
        (0, mine, edges1, lat1, rim1),
        (1, state2, edges2, lat2, rim2),
    )

    def send(exchange):
        step, *refs = exchange
        for index, (dlat, _) in enumerate(MESSAGES):
            guarded(dlat, lambda index=index: message(step, index, *refs).start())

    def receive(exchange, indices):
        step, *refs = exchange
        for index in indices:
            dlat = MESSAGES[index][0]
            guarded(-dlat, lambda index=index: message(step, index, *refs).wait_recv())

    def settle(exchange):
        step, *refs = exchange
        for index, (dlat, _) in enumerate(MESSAGES):
            guarded(dlat, lambda index=index: message(step, index, *refs).wait_send())

    send(exchanges[0])

    spread_w = jnp.broadcast_to(
        lift_w[0].astype(f32)[:, None, :], (2 * variables, rows, c0)
    ).reshape(2 * used, c0)
    row_of = lax.rem(lax.broadcasted_iota(jnp.int32, (lanes, c0), 0), rows)
    for part in range(2):
        piece = spread_w[part * used : (part + 1) * used]
        if lanes > used:
            piece = jnp.concatenate([piece, jnp.zeros((lanes - used, c0), f32)], axis=0)
        for r in range(rows):
            wlift[
                r // 2, part * lanes : (part + 1) * lanes, (r % 2) * c0 : (r % 2 + 1) * c0
            ] = jnp.where(row_of == r, piece, 0.0).astype(bf16)
    v_id = lax.broadcasted_iota(jnp.int32, (variables, lanes), 0)
    l_id = lax.broadcasted_iota(jnp.int32, (variables, lanes), 1)
    spreading = jnp.where((l_id >= v_id * rows) & (l_id < (v_id + 1) * rows), 1.0, 0.0).astype(bf16)
    spread_h = dot(head[0], spreading)
    lane_row = lax.rem(lax.broadcasted_iota(jnp.int32, (c0, lanes), 1), rows)
    for r in range(rows):
        whead[r * c0 : (r + 1) * c0, :] = jnp.where(lane_row == r, spread_h, 0.0).astype(bf16)
    expand_w = expand[0]
    shrink_w = jnp.concatenate([shrink[0], shrink[0]], axis=1)

    def inside(index):
        return jnp.logical_not(
            ((index < 0) & (lat == 0)) | ((index >= pairs) & (lat == n_lat - 1))
        )

    def masked(index, value):
        return jnp.where(inside(index), value, 0.0)

    def keep_fine(buffer, index, even, odd):
        buffer[0, index] = pltpu.roll(odd, 1, 0).astype(bf16)
        buffer[1, index] = even.astype(bf16)
        buffer[2, index] = odd.astype(bf16)
        buffer[3, index] = pltpu.roll(even, wide - 1, 0).astype(bf16)

    def keep_coarse(buffer, index, value):
        buffer[0, index] = pltpu.roll(value, 1, 0).astype(bf16)
        buffer[1, index] = value.astype(bf16)
        buffer[2, index] = pltpu.roll(value, wide - 1, 0).astype(bf16)

    def fine_window(buffer, index):
        def row(variant, q):
            at = index + (0, 1, 1, 2)[q]
            lane = (c0, 0, c0, 0)[q]
            return buffer[variant, at, :, lane : lane + c0]

        return jnp.concatenate(
            [
                jnp.concatenate([row(v + b, q) for q in range(4) for b in range(3)], axis=1)
                for v in range(2)
            ],
            axis=0,
        )

    def coarse_window(buffer, index):
        return jnp.concatenate(
            [buffer[b, index + a] for a in range(3) for b in range(3)], axis=1
        )

    def network(state_of, exchange):
        def assemble(slot):
            middle, left, right = state_of(slot)
            middle, left, right = (x.astype(f32) for x in (middle, left, right))
            cells[slot] = jnp.concatenate(
                [
                    left[:HALO],
                    middle[:half],
                    right[:HALO],
                    left[HALO:],
                    middle[half:],
                    right[HALO:],
                ],
                axis=0,
            ).astype(bf16)

        def lift_slot(slot):
            assemble(slot)

            def lift(p, carry):
                value = silu(dot(cells[slot], wlift[p]) + shift[...])
                if slot != 1:
                    value = masked((slot - 1) * pairs + p, value)
                keep_fine(lifted, slot * pairs + p, value[:wide], value[wide:])
                return carry

            lax.fori_loop(0, pairs, lift, 0)

        receive(exchange, (0, 1))
        lift_slot(1)
        receive(exchange, range(2, len(MESSAGES)))
        lift_slot(0)
        lift_slot(2)

        def down(step, carry):
            n = 2
            acc = dot(
                jnp.concatenate([fine_window(lifted, step * n + k) for k in range(n)], axis=0),
                w0a[...].reshape(12 * c0, 2 * c0),
            )
            value = silu(acc).astype(bf16)
            for k in range(n):
                index = step * n + k
                even = value[2 * k * wide : (2 * k + 1) * wide]
                odd = value[(2 * k + 1) * wide : (2 * k + 2) * wide]
                first[index, 0] = even
                first[index, 1] = odd
                total = even.astype(f32) + odd.astype(f32)
                pooled = ((total[:, :c0] + total[:, c0:]) * 0.25).astype(bf16)
                keep_coarse(widened, index, masked(index - (pairs - 1), dot(pooled, expand_w)))
            return carry

        if exchange[0] == 0:
            copies[0].wait()
            copies[1].wait()
        lax.fori_loop(0, (3 * pairs - 2) // 2, down, 0)

        def coarse_a(step, carry):
            n = 4
            acc = dot(
                jnp.concatenate([coarse_window(widened, step * n + k) for k in range(n)], axis=0),
                w1a[...].reshape(9 * w1a.shape[1], w1a.shape[2]),
            )
            value = silu(acc)
            for k in range(n):
                index = step * n + k
                keep_coarse(
                    inner, index, masked(index - (pairs - 2), value[k * wide : (k + 1) * wide])
                )
            return carry

        if exchange[0] == 0:
            copies[2].wait()
        lax.fori_loop(0, (3 * pairs - 4) // 4, coarse_a, 0)

        def coarse_b(step, carry):
            n = 3
            acc = dot(
                jnp.concatenate([coarse_window(inner, step * n + k) for k in range(n)], axis=0),
                w1b[...].reshape(9 * w1b.shape[1], w1b.shape[2]),
            )
            skip = jnp.concatenate([widened[1, step * n + k + 2] for k in range(n)], axis=0)
            projected = dot((silu(acc) + skip.astype(f32)).astype(bf16), shrink_w)
            for k in range(n):
                index = step * n + k
                piece = projected[k * wide : (k + 1) * wide]
                even = masked(index - 1, piece + first[index + 2, 0].astype(f32))
                odd = masked(index - 1, piece + first[index + 2, 1].astype(f32))
                keep_fine(merged, index, even, odd)
            return carry

        if exchange[0] == 0:
            copies[3].wait()
        lax.fori_loop(0, (pairs + 2) // 3, coarse_b, 0)

        def up(step, carry):
            n = 2
            acc = dot(
                jnp.concatenate([fine_window(merged, step * n + k) for k in range(n)], axis=0),
                w0b[...].reshape(12 * c0, 2 * c0),
            )
            value = silu(acc).astype(bf16)
            for k in range(n):
                last[step * n + k] = value[2 * k * wide : (2 * k + 2) * wide]
            return carry

        if exchange[0] == 0:
            copies[4].wait()
            copies[5].wait()
        lax.fori_loop(0, pairs // 2, up, 0)
        result = dot(jnp.concatenate([last[p] for p in range(pairs)], axis=1), whead[...])
        return jnp.concatenate(
            [result[HALO : HALO + half], result[wide + HALO : wide + HALO + half]], axis=0
        )

    def first_state(slot):
        middle = mine[...] if slot == 1 else lat1[0 if slot == 0 else 1]
        return middle, rim1[0, slot], rim1[1, slot]

    def second_state(slot):
        other = first_state(slot)
        middle = state2[...] if slot == 1 else lat2[0 if slot == 0 else 1]
        new = (middle, rim2[0, slot], rim2[1, slot])
        return tuple(
            jnp.concatenate([a, b[:, lanes:]], axis=1) for a, b in zip(new, other)
        )

    gains = jnp.concatenate([gain[...], gain[...]], axis=1)
    shift[...] = jnp.where(diffuse, high[3], 0.0).astype(f32) * gains
    first_out = network(first_state, exchanges[0])
    settle(exchanges[0])

    swap = pltpu.make_async_remote_copy(
        src_ref=finished,
        dst_ref=arrived,
        send_sem=swap_s,
        recv_sem=swap_r,
        device_id=partner,
        device_id_type=MESH,
    )

    @pl.when(jnp.logical_not(diffuse))
    def _():
        finished[...] = straight(first_out.astype(bf16)).astype(bf16)
        swap.start()

    @pl.when(diffuse)
    def _():
        noisy = sigma_high * given_t[...]
        first_denoised = high[1] * noisy + high[2] * first_out
        fresh = noisy + (sigma_low - sigma_high) / sigma_high * (noisy - first_denoised)
        moved[...] = fresh
        second_input = low[0] * fresh
        state2[...] = second_input.astype(bf16)
        borders(second_input, edges2)
        send(exchanges[1])
        shift[...] = low[3] * gains
        second_out = network(second_state, exchanges[1])
        second_denoised = low[1] * moved[...] + low[2] * second_out
        sample = mine[:, lanes:].astype(f32) + second_denoised
        finished[...] = straight(sample.astype(bf16)).astype(bf16)
        swap.start()
        settle(exchanges[1])

    swap.wait()
    out[0] = arrived[...].astype(f32).reshape(variables, rows, cols).astype(bf16)


def on_device(
    n_lat,
    n_lon,
    start,
    prior_mean,
    lift_w,
    noise_gain,
    conv0a,
    expand,
    conv1a,
    conv1b,
    shrink,
    conv0b,
    head,
):
    variables, rows, cols = prior_mean.shape
    c0, c1 = expand.shape[1:]
    pairs = rows // 2
    half = cols // 2
    wide = half + 2 * HALO
    lanes = -(-variables * rows // 128) * 128
    used = variables * rows
    assert pairs == 4 and 2 * c0 == c1
    split = (1, 3, 3, c0, c0)
    vmem = pl.BlockSpec(memory_space=pltpu.VMEM)
    hbm = pl.BlockSpec(memory_space=pl.ANY)
    scratch = [
        pltpu.VMEM((4, 3, c0, 2 * c0), bf16),
        pltpu.VMEM((4, 3, c0, 2 * c0), bf16),
        pltpu.VMEM((9, c1, c1), bf16),
        pltpu.VMEM((9, c1, c1), bf16),
        pltpu.VMEM((pairs, 2 * lanes, 2 * c0), bf16),
        pltpu.VMEM((rows * c0, lanes), bf16),
        pltpu.VMEM((cols, 2 * lanes), bf16),
        pltpu.VMEM((2, 2 * HALO, 2 * lanes), bf16),
        pltpu.VMEM((2, cols, 2 * lanes), bf16),
        pltpu.VMEM((2, 3, 2 * HALO, 2 * lanes), bf16),
        pltpu.VMEM((cols, lanes), bf16),
        pltpu.VMEM((2, 2 * HALO, lanes), bf16),
        pltpu.VMEM((2, cols, lanes), bf16),
        pltpu.VMEM((2, 3, 2 * HALO, lanes), bf16),
        pltpu.VMEM((cols, lanes), f32),
        pltpu.VMEM((cols, lanes), f32),
        pltpu.VMEM((1, 2 * c0), f32),
        pltpu.VMEM((3, 2 * wide, 2 * lanes), bf16),
        pltpu.VMEM((4, 3 * pairs, wide, 2 * c0), bf16),
        pltpu.VMEM((3 * pairs - 2, 2, wide, 2 * c0), bf16),
        pltpu.VMEM((3, 3 * pairs - 2, wide, c1), bf16),
        pltpu.VMEM((3, 3 * pairs - 4, wide, c1), bf16),
        pltpu.VMEM((4, pairs + 2, wide, 2 * c0), bf16),
        pltpu.VMEM((pairs, 2 * wide, 2 * c0), bf16),
        pltpu.VMEM((used, cols), bf16),
        pltpu.VMEM((used, cols), bf16),
        pltpu.SemaphoreType.DMA((6,)),
        pltpu.SemaphoreType.DMA((2, len(MESSAGES))),
        pltpu.SemaphoreType.DMA((2, len(MESSAGES))),
        pltpu.SemaphoreType.DMA,
        pltpu.SemaphoreType.DMA,
    ]
    return pl.pallas_call(
        functools.partial(kernel, n_lat, n_lon),
        out_shape=jax.ShapeDtypeStruct((1, variables, rows, cols), bf16),
        in_specs=[vmem, vmem, vmem, vmem, hbm, vmem, hbm, hbm, vmem, hbm, vmem],
        out_specs=vmem,
        scratch_shapes=scratch,
        compiler_params=pltpu.CompilerParams(
            collective_id=0, has_side_effects=True, vmem_limit_bytes=48 * 2**20
        ),
    )(
        start,
        prior_mean,
        lift_w,
        noise_gain,
        conv0a.reshape(split),
        expand,
        conv1a,
        conv1b,
        shrink,
        conv0b.reshape(split),
        head,
    )


def solution(mesh):
    placed = (
        P("section", None, "lat", "lon"),
        P(None, "lat", "lon"),
        P("section", None, None),
        P("section", None),
        P("section", None, None, None),
        P("section", None, None),
        P("section", None, None, None),
        P("section", None, None, None),
        P("section", None, None),
        P("section", None, None, None),
        P("section", None, None),
    )
    return jax.shard_map(
        functools.partial(on_device, mesh.shape["lat"], mesh.shape["lon"]),
        mesh=mesh,
        in_specs=placed,
        out_specs=P("section", None, "lat", "lon"),
        check_vma=False,
    )
```

```python
import functools
import math

import jax
import jax.numpy as jnp
from jax import lax
from jax.experimental import pallas as pl
from jax.experimental.pallas import tpu as pltpu
from jax.sharding import PartitionSpec as P

sigma_data = 0.5
sigma_high = 2.0
sigma_low = 0.5

MESH = pl.DeviceIdType.MESH
bf16 = jnp.bfloat16
f32 = jnp.float32

HALO = 8
MESSAGES = ((0, 1), (0, -1), (1, 1), (1, -1), (-1, 1), (-1, -1), (1, 0), (-1, 0))


def precondition(sigma):
    total = sigma * sigma + sigma_data * sigma_data
    return (
        1.0 / math.sqrt(total),
        sigma_data * sigma_data / total,
        sigma * sigma_data / math.sqrt(total),
        math.log(sigma) / 4.0,
    )


def silu(x):
    half = 0.5 * x
    return half + half * jnp.tanh(half)


def dot(a, b):
    return jnp.dot(a, b, preferred_element_type=f32)


def dot_nt(a, b):
    return lax.dot_general(a, b, (((1,), (1,)), ((), ())), preferred_element_type=f32)


def kernel(
    n_lat,
    n_lon,
    start_hbm,
    prior_hbm,
    lift_w_hbm,
    gain_hbm,
    conv0a,
    expand_hbm,
    conv1a,
    conv1b,
    shrink_hbm,
    conv0b,
    head_hbm,
    out,
    start,
    prior,
    lift_w,
    gain,
    expand,
    shrink,
    head,
    w0a,
    w0b,
    w1a,
    w1b,
    wlift,
    whead,
    mine,
    edges1,
    lat1,
    rim1,
    state2,
    edges2,
    lat2,
    rim2,
    given_t,
    moved,
    shift,
    cells,
    lifted,
    first,
    widened,
    inner,
    merged,
    last,
    finished,
    arrived,
    osem,
    wsem,
    ssem,
    rsem,
    swap_s,
    swap_r,
):
    section = lax.axis_index("section")
    lat = lax.axis_index("lat")
    lon = lax.axis_index("lon")
    diffuse = section == 1
    variables, rows, cols = prior.shape
    c0 = lift_w.shape[-1]
    half = cols // 2
    wide = half + 2 * HALO
    pairs = rows // 2
    used = variables * rows
    lanes = given_t.shape[1]
    high = precondition(sigma_high)
    low = precondition(sigma_low)

    def target(dlat, dlon):
        return (section, lat + dlat, lax.rem(lon + dlon + n_lon, n_lon))

    def present(dlat):
        if dlat < 0:
            return lat > 0
        return lat < n_lat - 1

    def guarded(dlat, action):
        if dlat == 0:
            action()
        else:
            pl.when(present(dlat))(action)

    partner = (1 - section, lat, lon)

    small = [
        pltpu.make_async_copy(source, landing, osem.at[k])
        for k, (source, landing) in enumerate(
            (
                (start_hbm.at[0], start),
                (prior_hbm, prior),
                (lift_w_hbm.at[0], lift_w),
                (gain_hbm, gain),
                (head_hbm.at[0], head),
                (expand_hbm.at[0], expand),
                (shrink_hbm.at[0], shrink),
            )
        )
    ]
    for copy in small:
        copy.start()

    barrier = pltpu.get_barrier_semaphore()
    pl.semaphore_signal(barrier, inc=1, device_id=partner, device_id_type=MESH)
    for dlat, dlon in MESSAGES:
        guarded(
            dlat,
            functools.partial(
                pl.semaphore_signal,
                barrier,
                inc=1,
                device_id=target(dlat, dlon),
                device_id_type=MESH,
            ),
        )

    copies = [
        pltpu.make_async_copy(
            conv0a.at[0], w0a.at[pl.ds(0, 3), :, :, pl.ds(0, c0)], wsem.at[0]
        ),
        pltpu.make_async_copy(
            conv0a.at[0], w0a.at[pl.ds(1, 3), :, :, pl.ds(c0, c0)], wsem.at[1]
        ),
        pltpu.make_async_copy(conv1a.at[0], w1a, wsem.at[2]),
        pltpu.make_async_copy(conv1b.at[0], w1b, wsem.at[3]),
        pltpu.make_async_copy(
            conv0b.at[0], w0b.at[pl.ds(0, 3), :, :, pl.ds(0, c0)], wsem.at[4]
        ),
        pltpu.make_async_copy(
            conv0b.at[0], w0b.at[pl.ds(1, 3), :, :, pl.ds(c0, c0)], wsem.at[5]
        ),
    ]
    for copy in copies:
        copy.start()
    for folded in (w0a, w0b):
        blank = jnp.zeros((3, c0, c0), bf16)
        folded[3, :, :, 0:c0] = blank
        folded[0, :, :, c0 : 2 * c0] = blank

    i = lax.broadcasted_iota(jnp.int32, (cols, cols), 0)
    j = lax.broadcasted_iota(jnp.int32, (cols, cols), 1)
    order = jnp.where(
        j == jnp.where(i < half, 2 * i, 2 * (i - half) + 1), 1.0, 0.0
    ).astype(bf16)

    def turned(x):
        flat = x.reshape(used, cols)
        if lanes > used:
            flat = jnp.concatenate([flat, jnp.zeros((lanes - used, cols), f32)], axis=0)
        return dot_nt(order, flat.astype(bf16))

    def straight(y):
        a = lax.broadcasted_iota(jnp.int32, (lanes, lanes), 0)
        b = lax.broadcasted_iota(jnp.int32, (lanes, lanes), 1)
        eye = jnp.where(a == b, 1.0, 0.0).astype(bf16)
        return dot(dot_nt(eye, y).astype(bf16), order)[:used]

    def borders(t, edges):
        edges[0] = jnp.concatenate([t[half - HALO : half], t[cols - HALO : cols]], axis=0).astype(bf16)
        edges[1] = jnp.concatenate([t[0:HALO], t[half : half + HALO]], axis=0).astype(bf16)

    small[0].wait()
    small[1].wait()
    given = start[...].astype(f32)
    scale = jnp.where(diffuse, high[0] * sigma_high, 1.0).astype(f32)
    state = turned(scale * given)
    prior_t = turned(prior[...].astype(f32))
    given_t[...] = turned(given)
    full = jnp.concatenate([state, prior_t], axis=1)
    mine[...] = full.astype(bf16)
    borders(full, edges1)

    pl.semaphore_wait(
        barrier,
        3 + jnp.where(lat > 0, 3, 0) + jnp.where(lat < n_lat - 1, 3, 0),
    )

    def message(step, index, block, edges, lat_in, rim_in):
        dlat, dlon = MESSAGES[index]
        if dlon == 0:
            source, landing = block, lat_in.at[0 if dlat > 0 else 1]
        else:
            side = 0 if dlon > 0 else 1
            source, landing = edges.at[side], rim_in.at[side, 1 - dlat]
        return pltpu.make_async_remote_copy(
            src_ref=source,
            dst_ref=landing,
            send_sem=ssem.at[step, index],
            recv_sem=rsem.at[step, index],
            device_id=target(dlat, dlon),
            device_id_type=MESH,
        )

    exchanges = (
        (0, mine, edges1, lat1, rim1),
        (1, state2, edges2, lat2, rim2),
    )

    def send(exchange):
        step, *refs = exchange
        for index, (dlat, _) in enumerate(MESSAGES):
            guarded(dlat, lambda index=index: message(step, index, *refs).start())

    def receive(exchange, indices):
        step, *refs = exchange
        for index in indices:
            dlat = MESSAGES[index][0]
            guarded(-dlat, lambda index=index: message(step, index, *refs).wait_recv())

    def settle(exchange):
        step, *refs = exchange
        for index, (dlat, _) in enumerate(MESSAGES):
            guarded(dlat, lambda index=index: message(step, index, *refs).wait_send())

    send(exchanges[0])

    for copy in small[2:]:
        copy.wait()
    spread_w = jnp.broadcast_to(
        lift_w[...].astype(f32)[:, None, :], (2 * variables, rows, c0)
    ).reshape(2 * used, c0)
    row_of = lax.rem(lax.broadcasted_iota(jnp.int32, (lanes, c0), 0), rows)
    for part in range(2):
        piece = spread_w[part * used : (part + 1) * used]
        if lanes > used:
            piece = jnp.concatenate([piece, jnp.zeros((lanes - used, c0), f32)], axis=0)
        for r in range(rows):
            wlift[
                r // 2, part * lanes : (part + 1) * lanes, (r % 2) * c0 : (r % 2 + 1) * c0
            ] = jnp.where(row_of == r, piece, 0.0).astype(bf16)
    v_id = lax.broadcasted_iota(jnp.int32, (variables, lanes), 0)
    l_id = lax.broadcasted_iota(jnp.int32, (variables, lanes), 1)
    spreading = jnp.where((l_id >= v_id * rows) & (l_id < (v_id + 1) * rows), 1.0, 0.0).astype(bf16)
    spread_h = lax.dot_general(
        head[...], spreading, (((0,), (0,)), ((), ())), preferred_element_type=f32
    )
    lane_row = lax.rem(lax.broadcasted_iota(jnp.int32, (c0, lanes), 1), rows)
    for r in range(rows):
        whead[r * c0 : (r + 1) * c0, :] = jnp.where(lane_row == r, spread_h, 0.0).astype(bf16)
    expand_w = expand[...]
    shrink_w = jnp.concatenate([shrink[...], shrink[...]], axis=1)

    def inside(index):
        return jnp.logical_not(
            ((index < 0) & (lat == 0)) | ((index >= pairs) & (lat == n_lat - 1))
        )

    def masked(index, value):
        if 0 <= index < pairs:
            return value
        return jnp.where(inside(index), value, 0.0)

    def keep_fine(buffer, index, even, odd):
        buffer[0, index] = pltpu.roll(odd, 1, 0).astype(bf16)
        buffer[1, index] = even.astype(bf16)
        buffer[2, index] = odd.astype(bf16)
        buffer[3, index] = pltpu.roll(even, wide - 1, 0).astype(bf16)

    def keep_coarse(buffer, index, value):
        buffer[0, index] = pltpu.roll(value, 1, 0).astype(bf16)
        buffer[1, index] = value.astype(bf16)
        buffer[2, index] = pltpu.roll(value, wide - 1, 0).astype(bf16)

    def fine_window(buffer, index):
        def row(variant, q):
            at = index + (0, 1, 1, 2)[q]
            lane = (c0, 0, c0, 0)[q]
            return buffer[variant, at, :, lane : lane + c0]

        return jnp.concatenate(
            [
                jnp.concatenate([row(v + b, q) for q in range(4) for b in range(3)], axis=1)
                for v in range(2)
            ],
            axis=0,
        )

    def coarse_window(buffer, index):
        return jnp.concatenate(
            [buffer[b, index + a] for a in range(3) for b in range(3)], axis=1
        )

    def network(state_of, exchange):
        def assemble(slot):
            middle, left, right = state_of(slot)
            middle, left, right = (x.astype(f32) for x in (middle, left, right))
            cells[slot] = jnp.concatenate(
                [
                    left[:HALO],
                    middle[:half],
                    right[:HALO],
                    left[HALO:],
                    middle[half:],
                    right[HALO:],
                ],
                axis=0,
            ).astype(bf16)

        def lift_slot(slot):
            assemble(slot)

            def lift(p):
                value = silu(dot(cells[slot], wlift[p]) + shift[...])
                value = masked((slot - 1) * pairs + p, value)
                keep_fine(lifted, slot * pairs + p, value[:wide], value[wide:])

            for p in range(pairs):
                lift(p)

        receive(exchange, (0, 1))
        lift_slot(1)

        def down(step):
            n = 2
            acc = dot(
                jnp.concatenate([fine_window(lifted, step * n + k) for k in range(n)], axis=0),
                w0a[...].reshape(12 * c0, 2 * c0),
            )
            value = silu(acc).astype(bf16)
            for k in range(n):
                index = step * n + k
                even = value[2 * k * wide : (2 * k + 1) * wide]
                odd = value[(2 * k + 1) * wide : (2 * k + 2) * wide]
                first[index, 0] = even
                first[index, 1] = odd
                total = even.astype(f32) + odd.astype(f32)
                pooled = ((total[:, :c0] + total[:, c0:]) * 0.25).astype(bf16)
                keep_coarse(widened, index, masked(index - (pairs - 1), dot(pooled, expand_w)))

        if exchange[0] == 0:
            copies[0].wait()
            copies[1].wait()
        down(pairs // 2)
        receive(exchange, range(2, len(MESSAGES)))
        lift_slot(0)
        lift_slot(2)
        for step in range((3 * pairs - 2) // 2):
            if step != pairs // 2:
                down(step)

        def coarse_a(step):
            n = 4
            acc = dot(
                jnp.concatenate([coarse_window(widened, step * n + k) for k in range(n)], axis=0),
                w1a[...].reshape(9 * w1a.shape[1], w1a.shape[2]),
            )
            value = silu(acc)
            for k in range(n):
                index = step * n + k
                keep_coarse(
                    inner, index, masked(index - (pairs - 2), value[k * wide : (k + 1) * wide])
                )

        if exchange[0] == 0:
            copies[2].wait()
        for step in range((3 * pairs - 4) // 4):
            coarse_a(step)

        def coarse_b(step):
            n = 3
            acc = dot(
                jnp.concatenate([coarse_window(inner, step * n + k) for k in range(n)], axis=0),
                w1b[...].reshape(9 * w1b.shape[1], w1b.shape[2]),
            )
            skip = jnp.concatenate([widened[1, step * n + k + 2] for k in range(n)], axis=0)
            projected = dot((silu(acc) + skip.astype(f32)).astype(bf16), shrink_w)
            for k in range(n):
                index = step * n + k
                piece = projected[k * wide : (k + 1) * wide]
                even = masked(index - 1, piece + first[index + 2, 0].astype(f32))
                odd = masked(index - 1, piece + first[index + 2, 1].astype(f32))
                keep_fine(merged, index, even, odd)

        if exchange[0] == 0:
            copies[3].wait()
        for step in range((pairs + 2) // 3):
            coarse_b(step)

        def up(step):
            n = 2
            acc = dot(
                jnp.concatenate([fine_window(merged, step * n + k) for k in range(n)], axis=0),
                w0b[...].reshape(12 * c0, 2 * c0),
            )
            value = silu(acc).astype(bf16)
            for k in range(n):
                last[step * n + k] = value[2 * k * wide : (2 * k + 2) * wide]

        if exchange[0] == 0:
            copies[4].wait()
            copies[5].wait()
        for step in range(pairs // 2):
            up(step)
        result = dot(jnp.concatenate([last[p] for p in range(pairs)], axis=1), whead[...])
        return jnp.concatenate(
            [result[HALO : HALO + half], result[wide + HALO : wide + HALO + half]], axis=0
        )

    def first_state(slot):
        middle = mine[...] if slot == 1 else lat1[0 if slot == 0 else 1]
        return middle, rim1[0, slot], rim1[1, slot]

    def second_state(slot):
        other = first_state(slot)
        middle = state2[...] if slot == 1 else lat2[0 if slot == 0 else 1]
        new = (middle, rim2[0, slot], rim2[1, slot])
        return tuple(
            jnp.concatenate([a, b[:, lanes:]], axis=1) for a, b in zip(new, other)
        )

    gains = jnp.concatenate([gain[...], gain[...]], axis=1)
    shift[...] = jnp.where(diffuse, high[3], 0.0).astype(f32) * gains
    first_out = network(first_state, exchanges[0])
    settle(exchanges[0])

    swap = pltpu.make_async_remote_copy(
        src_ref=finished,
        dst_ref=arrived,
        send_sem=swap_s,
        recv_sem=swap_r,
        device_id=partner,
        device_id_type=MESH,
    )

    @pl.when(jnp.logical_not(diffuse))
    def _():
        finished[...] = straight(first_out.astype(bf16)).astype(bf16)
        swap.start()

    @pl.when(diffuse)
    def _():
        noisy = sigma_high * given_t[...]
        first_denoised = high[1] * noisy + high[2] * first_out
        fresh = noisy + (sigma_low - sigma_high) / sigma_high * (noisy - first_denoised)
        moved[...] = fresh
        second_input = low[0] * fresh
        state2[...] = second_input.astype(bf16)
        borders(second_input, edges2)
        send(exchanges[1])
        shift[...] = low[3] * gains
        second_out = network(second_state, exchanges[1])
        second_denoised = low[1] * moved[...] + low[2] * second_out
        sample = mine[:, lanes:].astype(f32) + second_denoised
        finished[...] = straight(sample.astype(bf16)).astype(bf16)
        swap.start()
        settle(exchanges[1])

    swap.wait()
    out[0] = arrived[...].astype(f32).reshape(variables, rows, cols).astype(bf16)


def on_device(
    n_lat,
    n_lon,
    start,
    prior_mean,
    lift_w,
    noise_gain,
    conv0a,
    expand,
    conv1a,
    conv1b,
    shrink,
    conv0b,
    head,
):
    variables, rows, cols = prior_mean.shape
    c0, c1 = expand.shape[1:]
    pairs = rows // 2
    half = cols // 2
    wide = half + 2 * HALO
    lanes = -(-variables * rows // 128) * 128
    used = variables * rows
    assert pairs == 4 and 2 * c0 == c1
    split = (1, 3, 3, c0, c0)
    vmem = pl.BlockSpec(memory_space=pltpu.VMEM)
    head_t = jnp.swapaxes(head, 1, 2)
    hbm = pl.BlockSpec(memory_space=pl.ANY)
    scratch = [
        pltpu.VMEM(start.shape[1:], bf16),
        pltpu.VMEM(prior_mean.shape, bf16),
        pltpu.VMEM(lift_w.shape[1:], bf16),
        pltpu.VMEM(noise_gain.shape, f32),
        pltpu.VMEM(expand.shape[1:], bf16),
        pltpu.VMEM(shrink.shape[1:], bf16),
        pltpu.VMEM(head_t.shape[1:], bf16),
        pltpu.VMEM((4, 3, c0, 2 * c0), bf16),
        pltpu.VMEM((4, 3, c0, 2 * c0), bf16),
        pltpu.VMEM((9, c1, c1), bf16),
        pltpu.VMEM((9, c1, c1), bf16),
        pltpu.VMEM((pairs, 2 * lanes, 2 * c0), bf16),
        pltpu.VMEM((rows * c0, lanes), bf16),
        pltpu.VMEM((cols, 2 * lanes), bf16),
        pltpu.VMEM((2, 2 * HALO, 2 * lanes), bf16),
        pltpu.VMEM((2, cols, 2 * lanes), bf16),
        pltpu.VMEM((2, 3, 2 * HALO, 2 * lanes), bf16),
        pltpu.VMEM((cols, lanes), bf16),
        pltpu.VMEM((2, 2 * HALO, lanes), bf16),
        pltpu.VMEM((2, cols, lanes), bf16),
        pltpu.VMEM((2, 3, 2 * HALO, lanes), bf16),
        pltpu.VMEM((cols, lanes), f32),
        pltpu.VMEM((cols, lanes), f32),
        pltpu.VMEM((1, 2 * c0), f32),
        pltpu.VMEM((3, 2 * wide, 2 * lanes), bf16),
        pltpu.VMEM((4, 3 * pairs, wide, 2 * c0), bf16),
        pltpu.VMEM((3 * pairs - 2, 2, wide, 2 * c0), bf16),
        pltpu.VMEM((3, 3 * pairs - 2, wide, c1), bf16),
        pltpu.VMEM((3, 3 * pairs - 4, wide, c1), bf16),
        pltpu.VMEM((4, pairs + 2, wide, 2 * c0), bf16),
        pltpu.VMEM((pairs, 2 * wide, 2 * c0), bf16),
        pltpu.VMEM((used, cols), bf16),
        pltpu.VMEM((used, cols), bf16),
        pltpu.SemaphoreType.DMA((7,)),
        pltpu.SemaphoreType.DMA((6,)),
        pltpu.SemaphoreType.DMA((2, len(MESSAGES))),
        pltpu.SemaphoreType.DMA((2, len(MESSAGES))),
        pltpu.SemaphoreType.DMA,
        pltpu.SemaphoreType.DMA,
    ]
    return pl.pallas_call(
        functools.partial(kernel, n_lat, n_lon),
        out_shape=jax.ShapeDtypeStruct((1, variables, rows, cols), bf16),
        in_specs=[hbm] * 11,
        out_specs=vmem,
        scratch_shapes=scratch,
        compiler_params=pltpu.CompilerParams(
            collective_id=0, has_side_effects=True, vmem_limit_bytes=60 * 2**20
        ),
    )(
        start,
        prior_mean,
        lift_w,
        noise_gain,
        conv0a.reshape(split),
        expand,
        conv1a,
        conv1b,
        shrink,
        conv0b.reshape(split),
        head_t,
    )


def solution(mesh):
    placed = (
        P("section", None, "lat", "lon"),
        P(None, "lat", "lon"),
        P("section", None, None),
        P("section", None),
        P("section", None, None, None),
        P("section", None, None),
        P("section", None, None, None),
        P("section", None, None, None),
        P("section", None, None),
        P("section", None, None, None),
        P("section", None, None),
    )
    return jax.shard_map(
        functools.partial(on_device, mesh.shape["lat"], mesh.shape["lon"]),
        mesh=mesh,
        in_specs=placed,
        out_specs=P("section", None, "lat", "lon"),
        check_vma=False,
    )
```

```python
import functools
import math

import jax
import jax.numpy as jnp
from jax import lax
from jax.experimental import pallas as pl
from jax.experimental.pallas import tpu as pltpu
from jax.sharding import PartitionSpec as P

sigma_data = 0.5
sigma_high = 2.0
sigma_low = 0.5

MESH = pl.DeviceIdType.MESH
bf16 = jnp.bfloat16
f32 = jnp.float32

HALO = 4


def precondition(sigma):
    total = sigma * sigma + sigma_data * sigma_data
    return (
        1.0 / math.sqrt(total),
        sigma_data * sigma_data / total,
        sigma * sigma_data / math.sqrt(total),
        math.log(sigma) / 4.0,
    )


def silu(x):
    half = 0.5 * x
    return half + half * jnp.tanh(half)


def dot(a, b):
    return jnp.dot(a, b, preferred_element_type=f32)


def dot_nt(a, b):
    return lax.dot_general(a, b, (((1,), (1,)), ((), ())), preferred_element_type=f32)


def kernel(
    n_lat,
    n_lon,
    start_hbm,
    prior_hbm,
    lift_w_hbm,
    gain_hbm,
    conv0a,
    expand_hbm,
    conv1a,
    conv1b,
    shrink_hbm,
    conv0b,
    head_hbm,
    out,
    start,
    prior,
    lift_w,
    gain,
    expand,
    shrink,
    head,
    w0a,
    w0b,
    w1a,
    w1b,
    wlift,
    whead,
    outbox,
    inbox,
    rims_out,
    rims_in,
    edges_out,
    edges_in,
    given_t,
    moved,
    shift,
    cells,
    lifted,
    first,
    widened,
    inner,
    merged,
    last,
    finished,
    arrived,
    osem,
    wsem,
    box_s,
    box_r,
    rim_s,
    rim_r,
    edge_s,
    edge_r,
    swap_s,
    swap_r,
):
    section = lax.axis_index("section")
    lat = lax.axis_index("lat")
    lon = lax.axis_index("lon")
    diffuse = section == 1
    variables, rows, cols = prior.shape
    c0 = lift_w.shape[-1]
    half = cols // 2
    own = half // n_lat
    wide = own + 2 * HALO
    slab = widened.shape[2]
    pairs = rows // 2
    total = n_lat * pairs
    used = variables * rows
    lanes = given_t.shape[1]
    high = precondition(sigma_high)
    low = precondition(sigma_low)
    east = lax.rem(lon + 1, n_lon)
    west = lax.rem(lon + n_lon - 1, n_lon)
    final = n_lat - 1

    small = [
        pltpu.make_async_copy(source, landing, osem.at[k])
        for k, (source, landing) in enumerate(
            (
                (start_hbm.at[0], start),
                (prior_hbm, prior),
                (lift_w_hbm.at[0], lift_w),
                (gain_hbm, gain),
                (head_hbm.at[0], head),
                (expand_hbm.at[0], expand),
                (shrink_hbm.at[0], shrink),
            )
        )
    ]
    for copy in small:
        copy.start()

    barrier = pltpu.get_barrier_semaphore()

    def greet(device):
        pl.semaphore_signal(barrier, inc=1, device_id=device, device_id_type=MESH)

    for step in range(1, n_lat):
        greet((section, lax.rem(lat + step, n_lat), lon))
    for k in range(n_lat):
        greet((1 - section, k, lon))

    @pl.when(lat == 0)
    def _():
        for k in range(n_lat):
            greet((section, k, west))

    @pl.when(lat == final)
    def _():
        for k in range(n_lat):
            greet((section, k, east))

    copies = [
        pltpu.make_async_copy(
            conv0a.at[0], w0a.at[pl.ds(0, 3), :, :, pl.ds(0, c0)], wsem.at[0]
        ),
        pltpu.make_async_copy(
            conv0a.at[0], w0a.at[pl.ds(1, 3), :, :, pl.ds(c0, c0)], wsem.at[1]
        ),
        pltpu.make_async_copy(conv1a.at[0], w1a, wsem.at[2]),
        pltpu.make_async_copy(conv1b.at[0], w1b, wsem.at[3]),
        pltpu.make_async_copy(
            conv0b.at[0], w0b.at[pl.ds(0, 3), :, :, pl.ds(0, c0)], wsem.at[4]
        ),
        pltpu.make_async_copy(
            conv0b.at[0], w0b.at[pl.ds(1, 3), :, :, pl.ds(c0, c0)], wsem.at[5]
        ),
    ]
    for copy in copies:
        copy.start()
    for folded in (w0a, w0b):
        blank = jnp.zeros((3, c0, c0), bf16)
        folded[3, :, :, 0:c0] = blank
        folded[0, :, :, c0 : 2 * c0] = blank
    for padded in (lifted, widened, inner, merged):
        blank = jnp.zeros((3,) + padded.shape[2:], bf16)
        padded[:, 0] = blank
        padded[:, total + 1] = blank

    def pick(base, count, parity):
        i = lax.broadcasted_iota(jnp.int32, (count, cols), 0)
        j = lax.broadcasted_iota(jnp.int32, (count, cols), 1)
        return jnp.where(j == 2 * (base + i) + parity, 1.0, 0.0)

    picks = [pick(k * own - HALO, wide, parity) for k in range(n_lat) for parity in range(2)]
    rim_picks = [
        pick(base, 2 * HALO, parity) for base in (half - HALO, -HALO) for parity in range(2)
    ]
    order = jnp.concatenate(picks + rim_picks, axis=0).astype(bf16)

    def turned(x):
        flat = x.reshape(used, cols)
        if lanes > used:
            flat = jnp.concatenate([flat, jnp.zeros((lanes - used, cols), f32)], axis=0)
        return dot_nt(order, flat.astype(bf16))

    small[0].wait()
    small[1].wait()
    full = jnp.concatenate(
        [turned(start[...].astype(f32)), turned(prior[...].astype(f32))], axis=1
    ).astype(bf16)
    for k in range(n_lat):
        outbox[k] = full[2 * wide * k : 2 * wide * (k + 1)]
    for side in range(2):
        at = 2 * wide * n_lat + 4 * HALO * side
        rims_out[side] = full[at : at + 4 * HALO]

    pl.semaphore_wait(barrier, 2 * n_lat + 1)

    def rim(side, source):
        return pltpu.make_async_remote_copy(
            src_ref=rims_out.at[side],
            dst_ref=rims_in.at[side, source],
            send_sem=rim_s.at[side],
            recv_sem=rim_r.at[side, source],
            device_id=(section, 0, east) if side == 0 else (section, final, west),
            device_id_type=MESH,
        )

    def box(step, source):
        to = lax.rem(lat + step, n_lat)
        return pltpu.make_async_remote_copy(
            src_ref=outbox.at[to],
            dst_ref=inbox.at[source],
            send_sem=box_s.at[step - 1],
            recv_sem=box_r.at[step - 1],
            device_id=(section, to, lon),
            device_id_type=MESH,
        )

    for side in range(2):
        rim(side, lat).start()
    for step in range(1, n_lat):
        box(step, lat).start()
    inbox[lat] = outbox[lat]

    for copy in small[2:]:
        copy.wait()
    spread_w = jnp.broadcast_to(
        lift_w[...].astype(f32)[:, None, :], (2 * variables, rows, c0)
    ).reshape(2 * used, c0)
    row_of = lax.rem(lax.broadcasted_iota(jnp.int32, (lanes, c0), 0), rows)
    for part in range(2):
        piece = spread_w[part * used : (part + 1) * used]
        if lanes > used:
            piece = jnp.concatenate([piece, jnp.zeros((lanes - used, c0), f32)], axis=0)
        for r in range(rows):
            wlift[
                r // 2, part * lanes : (part + 1) * lanes, (r % 2) * c0 : (r % 2 + 1) * c0
            ] = jnp.where(row_of == r, piece, 0.0).astype(bf16)
    v_id = lax.broadcasted_iota(jnp.int32, (variables, lanes), 0)
    l_id = lax.broadcasted_iota(jnp.int32, (variables, lanes), 1)
    spreading = jnp.where((l_id >= v_id * rows) & (l_id < (v_id + 1) * rows), 1.0, 0.0).astype(bf16)
    spread_h = lax.dot_general(
        head[...], spreading, (((0,), (0,)), ((), ())), preferred_element_type=f32
    )
    lane_row = lax.rem(lax.broadcasted_iota(jnp.int32, (c0, lanes), 1), rows)
    for r in range(rows):
        whead[r * c0 : (r + 1) * c0, :] = jnp.where(lane_row == r, spread_h, 0.0).astype(bf16)
    expand_w = expand[...]
    shrink_w = jnp.concatenate([shrink[...], shrink[...]], axis=1)
    gains = jnp.concatenate([gain[...], gain[...]], axis=1)
    shift[...] = jnp.where(diffuse, high[3], 0.0).astype(f32) * gains

    for step in range(1, n_lat):
        box(step, lax.rem(lat + n_lat - step, n_lat)).wait_recv()

    @pl.when(lat == 0)
    def _():
        for k in range(n_lat):
            rim(0, k).wait_recv()

    @pl.when(lat == final)
    def _():
        for k in range(n_lat):
            rim(1, k).wait_recv()

    scale = jnp.where(diffuse, high[0] * sigma_high, 1.0).astype(f32)
    near = lax.broadcasted_iota(jnp.int32, (2 * HALO, lanes), 0) < HALO
    depth = 2 * HALO
    for k in range(n_lat):
        block = inbox[k].astype(f32)
        left = jnp.where(lat == 0, rims_in[0, k].astype(f32), 0.0)
        right = jnp.where(lat == final, rims_in[1, k].astype(f32), 0.0)
        whole = []
        for parity in range(2):
            part = block[parity * wide : (parity + 1) * wide]
            rim_rows = slice(parity * depth, (parity + 1) * depth)
            whole += [
                part[:depth] + left[rim_rows],
                part[depth : wide - depth],
                part[wide - depth :] + right[rim_rows],
            ]
        whole = jnp.concatenate(whole, axis=0)
        place = slice(2 * wide * k, 2 * wide * (k + 1))
        given_t[place] = whole[:, :lanes]
        cells[place, :lanes] = (scale * whole[:, :lanes]).astype(bf16)
        cells[place, lanes:] = whole[:, lanes:].astype(bf16)

    def keep_fine(buffer, index, value):
        even, odd = value[:wide], value[wide:]
        buffer[0, index] = jnp.concatenate([pltpu.roll(odd, 1, 0), even], axis=0).astype(bf16)
        buffer[1, index] = value.astype(bf16)
        buffer[2, index] = jnp.concatenate(
            [odd, pltpu.roll(even, wide - 1, 0)], axis=0
        ).astype(bf16)

    def keep_coarse(buffer, index, value):
        buffer[0, index] = pltpu.roll(value, 1, 0).astype(bf16)
        buffer[1, index] = value.astype(bf16)
        buffer[2, index] = pltpu.roll(value, slab - 1, 0).astype(bf16)

    def fine_window(buffer, index):
        pieces = []
        for at, lane in ((0, c0), (1, 0), (1, c0), (2, 0)):
            pieces += [buffer[b, index + at, :, lane : lane + c0] for b in range(3)]
        return jnp.concatenate(pieces, axis=1)

    def coarse_window(buffer, index):
        return jnp.concatenate(
            [buffer[b, index + a] for a in range(3) for b in range(3)], axis=1
        )

    def stacked(window, buffer, indices):
        return jnp.concatenate([window(buffer, index) for index in indices], axis=0)

    def groups(count):
        return [range(at, at + count) for at in range(0, total, count)]

    def network(loading):
        for p in range(pairs):
            value = silu(dot(cells[...], wlift[p]) + shift[...])
            for k in range(n_lat):
                keep_fine(
                    lifted, k * pairs + p + 1, value[2 * wide * k : 2 * wide * (k + 1)]
                )
        if loading:
            copies[0].wait()
            copies[1].wait()
        for group in groups(pairs):
            acc = dot(stacked(fine_window, lifted, group), w0a[...].reshape(12 * c0, 2 * c0))
            value = silu(acc).astype(bf16)
            pooled = []
            for k, index in enumerate(group):
                piece = value[2 * wide * k : 2 * wide * (k + 1)]
                first[index] = piece
                piece = piece.astype(f32)
                piece = piece[:wide] + piece[wide:]
                pooled.append((piece[:, :c0] + piece[:, c0:]) * 0.25)
                if slab > wide:
                    pooled.append(jnp.zeros((slab - wide, c0), f32))
            result = dot(jnp.concatenate(pooled, axis=0).astype(bf16), expand_w)
            for k, index in enumerate(group):
                keep_coarse(widened, index + 1, result[slab * k : slab * (k + 1)])
        if loading:
            copies[2].wait()
        for group in groups(2 * pairs):
            acc = dot(
                stacked(coarse_window, widened, group),
                w1a[...].reshape(9 * w1a.shape[1], w1a.shape[2]),
            )
            value = silu(acc)
            for k, index in enumerate(group):
                keep_coarse(inner, index + 1, value[slab * k : slab * (k + 1)])
        if loading:
            copies[3].wait()
        for group in groups(2 * pairs):
            acc = dot(
                stacked(coarse_window, inner, group),
                w1b[...].reshape(9 * w1b.shape[1], w1b.shape[2]),
            )
            skip = jnp.concatenate([widened[1, index + 1] for index in group], axis=0)
            projected = dot((silu(acc) + skip.astype(f32)).astype(bf16), shrink_w)
            for k, index in enumerate(group):
                piece = projected[slab * k : slab * k + wide]
                keep_fine(
                    merged,
                    index + 1,
                    jnp.concatenate([piece, piece], axis=0) + first[index].astype(f32),
                )
        if loading:
            copies[4].wait()
            copies[5].wait()
        for group in groups(pairs):
            acc = dot(stacked(fine_window, merged, group), w0b[...].reshape(12 * c0, 2 * c0))
            value = silu(acc).astype(bf16)
            for k, index in enumerate(group):
                last[index] = value[2 * wide * k : 2 * wide * (k + 1)]
        return dot(
            jnp.concatenate(
                [
                    jnp.concatenate([last[index] for index in group], axis=1)
                    for group in groups(pairs)
                ],
                axis=0,
            ),
            whead[...],
        )

    def swap(to, source):
        return pltpu.make_async_remote_copy(
            src_ref=finished.at[to],
            dst_ref=arrived.at[source],
            send_sem=swap_s.at[to],
            recv_sem=swap_r.at[source],
            device_id=(1 - section, to, lon),
            device_id_type=MESH,
        )

    def hand_over(value):
        value = value.astype(bf16)
        for k in range(n_lat):
            finished[k] = value[2 * wide * k : 2 * wide * (k + 1)]
        for k in range(n_lat):
            swap(k, lat).start()

    first_out = network(True)
    for side in range(2):
        rim(side, lat).wait_send()
    for step in range(1, n_lat):
        box(step, lat).wait_send()

    @pl.when(jnp.logical_not(diffuse))
    def _():
        hand_over(first_out)

    @pl.when(diffuse)
    def _():
        noisy = sigma_high * given_t[...]
        first_denoised = high[1] * noisy + high[2] * first_out
        fresh = noisy + (sigma_low - sigma_high) / sigma_high * (noisy - first_denoised)
        moved[...] = fresh
        second_input = low[0] * fresh

        def part(k, parity):
            at = 2 * wide * k + wide * parity
            return second_input[at : at + wide]

        order_of = [(k, parity) for k in range(n_lat) for parity in range(2)]
        edges_out[0] = jnp.concatenate(
            [part(*at)[wide - depth :] for at in order_of], axis=0
        ).astype(bf16)
        edges_out[1] = jnp.concatenate([part(*at)[:depth] for at in order_of], axis=0).astype(bf16)

        to_east = (
            section,
            lax.rem(lat + 1, n_lat),
            lax.rem(lon + jnp.where(lat == final, 1, 0), n_lon),
        )
        to_west = (
            section,
            lax.rem(lat + n_lat - 1, n_lat),
            lax.rem(lon + n_lon - jnp.where(lat == 0, 1, 0), n_lon),
        )
        edges = [
            pltpu.make_async_remote_copy(
                src_ref=edges_out.at[side],
                dst_ref=edges_in.at[side],
                send_sem=edge_s.at[side],
                recv_sem=edge_r.at[side],
                device_id=(to_east, to_west)[side],
                device_id_type=MESH,
            )
            for side in range(2)
        ]
        for edge in edges:
            edge.start()
        shift[...] = low[3] * gains
        for edge in edges:
            edge.wait_recv()
        left = edges_in[0].astype(f32)
        right = edges_in[1].astype(f32)
        whole = []
        for n, at in enumerate(order_of):
            piece = part(*at)
            rim_rows = slice(depth * n, depth * (n + 1))
            whole += [
                jnp.where(near, left[rim_rows], piece[:depth]),
                piece[depth : wide - depth],
                jnp.where(near, piece[wide - depth :], right[rim_rows]),
            ]
        cells[:, :lanes] = jnp.concatenate(whole, axis=0).astype(bf16)
        second_out = network(False)
        second_denoised = low[1] * moved[...] + low[2] * second_out
        hand_over(cells[:, lanes:].astype(f32) + second_denoised)
        for edge in edges:
            edge.wait_send()

    def unpick(base):
        i = lax.broadcasted_iota(jnp.int32, (wide, cols), 0)
        j = lax.broadcasted_iota(jnp.int32, (wide, cols), 1)
        middle = (i >= HALO) & (i < wide - HALO)
        return [
            jnp.where(middle & (j == 2 * (base + i) + parity), 1.0, 0.0) for parity in range(2)
        ]

    back = jnp.concatenate(
        [piece for k in range(n_lat) for piece in unpick(k * own - HALO)], axis=0
    ).astype(bf16)
    a = lax.broadcasted_iota(jnp.int32, (lanes, lanes), 0)
    b = lax.broadcasted_iota(jnp.int32, (lanes, lanes), 1)
    eye = jnp.where(a == b, 1.0, 0.0).astype(bf16)
    for k in range(n_lat):
        swap(k, k).wait_recv()
    gathered = arrived[...].reshape(n_lat * 2 * wide, lanes)
    result = dot(dot_nt(eye, gathered).astype(bf16), back)[:used]
    out[0] = result.reshape(variables, rows, cols).astype(bf16)
    for k in range(n_lat):
        swap(k, lat).wait_send()


def on_device(
    n_lat,
    n_lon,
    start,
    prior_mean,
    lift_w,
    noise_gain,
    conv0a,
    expand,
    conv1a,
    conv1b,
    shrink,
    conv0b,
    head,
):
    variables, rows, cols = prior_mean.shape
    c0, c1 = expand.shape[1:]
    pairs = rows // 2
    total = n_lat * pairs
    wide = cols // 2 // n_lat + 2 * HALO
    slab = -(-wide // 16) * 16
    used = variables * rows
    lanes = -(-used // 128) * 128
    depth = 4 * HALO
    assert 2 * c0 == c1 and wide % 8 == 0 and n_lat % 2 == 0 and rows % 2 == 0
    split = (1, 3, 3, c0, c0)
    head_t = jnp.swapaxes(head, 1, 2)
    scratch = [
        pltpu.VMEM(start.shape[1:], bf16),
        pltpu.VMEM(prior_mean.shape, bf16),
        pltpu.VMEM(lift_w.shape[1:], bf16),
        pltpu.VMEM(noise_gain.shape, f32),
        pltpu.VMEM(expand.shape[1:], bf16),
        pltpu.VMEM(shrink.shape[1:], bf16),
        pltpu.VMEM(head_t.shape[1:], bf16),
        pltpu.VMEM((4, 3, c0, 2 * c0), bf16),
        pltpu.VMEM((4, 3, c0, 2 * c0), bf16),
        pltpu.VMEM((9, c1, c1), bf16),
        pltpu.VMEM((9, c1, c1), bf16),
        pltpu.VMEM((pairs, 2 * lanes, 2 * c0), bf16),
        pltpu.VMEM((rows * c0, lanes), bf16),
        pltpu.VMEM((n_lat, 2 * wide, 2 * lanes), bf16),
        pltpu.VMEM((n_lat, 2 * wide, 2 * lanes), bf16),
        pltpu.VMEM((2, depth, 2 * lanes), bf16),
        pltpu.VMEM((2, n_lat, depth, 2 * lanes), bf16),
        pltpu.VMEM((2, n_lat * depth, lanes), bf16),
        pltpu.VMEM((2, n_lat * depth, lanes), bf16),
        pltpu.VMEM((n_lat * 2 * wide, lanes), f32),
        pltpu.VMEM((n_lat * 2 * wide, lanes), f32),
        pltpu.VMEM((1, 2 * c0), f32),
        pltpu.VMEM((n_lat * 2 * wide, 2 * lanes), bf16),
        pltpu.VMEM((3, total + 2, 2 * wide, 2 * c0), bf16),
        pltpu.VMEM((total, 2 * wide, 2 * c0), bf16),
        pltpu.VMEM((3, total + 2, slab, c1), bf16),
        pltpu.VMEM((3, total + 2, slab, c1), bf16),
        pltpu.VMEM((3, total + 2, 2 * wide, 2 * c0), bf16),
        pltpu.VMEM((total, 2 * wide, 2 * c0), bf16),
        pltpu.VMEM((n_lat, 2 * wide, lanes), bf16),
        pltpu.VMEM((n_lat, 2 * wide, lanes), bf16),
        pltpu.SemaphoreType.DMA((7,)),
        pltpu.SemaphoreType.DMA((6,)),
        pltpu.SemaphoreType.DMA((n_lat - 1,)),
        pltpu.SemaphoreType.DMA((n_lat - 1,)),
        pltpu.SemaphoreType.DMA((2,)),
        pltpu.SemaphoreType.DMA((2, n_lat)),
        pltpu.SemaphoreType.DMA((2,)),
        pltpu.SemaphoreType.DMA((2,)),
        pltpu.SemaphoreType.DMA((n_lat,)),
        pltpu.SemaphoreType.DMA((n_lat,)),
    ]
    return pl.pallas_call(
        functools.partial(kernel, n_lat, n_lon),
        out_shape=jax.ShapeDtypeStruct((1, variables, rows, cols), bf16),
        in_specs=[pl.BlockSpec(memory_space=pl.ANY)] * 11,
        out_specs=pl.BlockSpec(memory_space=pltpu.VMEM),
        scratch_shapes=scratch,
        compiler_params=pltpu.CompilerParams(
            collective_id=0, has_side_effects=True, vmem_limit_bytes=60 * 2**20
        ),
    )(
        start,
        prior_mean,
        lift_w,
        noise_gain,
        conv0a.reshape(split),
        expand,
        conv1a,
        conv1b,
        shrink,
        conv0b.reshape(split),
        head_t,
    )


def solution(mesh):
    placed = (
        P("section", None, "lat", "lon"),
        P(None, "lat", "lon"),
        P("section", None, None),
        P("section", None),
        P("section", None, None, None),
        P("section", None, None),
        P("section", None, None, None),
        P("section", None, None, None),
        P("section", None, None),
        P("section", None, None, None),
        P("section", None, None),
    )
    return jax.shard_map(
        functools.partial(on_device, mesh.shape["lat"], mesh.shape["lon"]),
        mesh=mesh,
        in_specs=placed,
        out_specs=P("section", None, "lat", "lon"),
        check_vma=False,
    )
```

```python
import functools
import math

import jax
import jax.numpy as jnp
from jax import lax
from jax.experimental import pallas as pl
from jax.experimental.pallas import tpu as pltpu
from jax.sharding import PartitionSpec as P

sigma_data = 0.5
sigma_high = 2.0
sigma_low = 0.5

MESH = pl.DeviceIdType.MESH
bf16 = jnp.bfloat16
f32 = jnp.float32

HALO = 4


def precondition(sigma):
    total = sigma * sigma + sigma_data * sigma_data
    return (
        1.0 / math.sqrt(total),
        sigma_data * sigma_data / total,
        sigma * sigma_data / math.sqrt(total),
        math.log(sigma) / 4.0,
    )


def silu(x):
    half = 0.5 * x
    return half + half * jnp.tanh(half)


def dot(a, b):
    return jnp.dot(a, b, preferred_element_type=f32)


def dot_nt(a, b):
    return lax.dot_general(a, b, (((1,), (1,)), ((), ())), preferred_element_type=f32)


def kernel(
    n_lat,
    n_lon,
    start_hbm,
    prior_hbm,
    lift_w_hbm,
    gain_hbm,
    conv0a,
    expand_hbm,
    conv1a,
    conv1b,
    shrink_hbm,
    conv0b,
    head_hbm,
    out,
    start,
    prior,
    lift_w,
    gain,
    expand,
    shrink,
    head,
    w0a,
    w0b,
    w1a,
    w1b,
    wlift,
    whead,
    outbox,
    inbox,
    rims_out,
    rims_in,
    edges_out,
    edges_in,
    given_t,
    moved,
    shift,
    cells,
    lifted,
    first,
    widened,
    inner,
    merged,
    last,
    finished,
    arrived,
    osem,
    wsem,
    box_s,
    box_r,
    rim_s,
    rim_r,
    edge_s,
    edge_r,
    swap_s,
    swap_r,
):
    section = lax.axis_index("section")
    lat = lax.axis_index("lat")
    lon = lax.axis_index("lon")
    diffuse = section == 1
    variables, rows, cols = prior.shape
    c0 = lift_w.shape[-1]
    half = cols // 2
    own = half // n_lat
    wide = own + 2 * HALO
    slab = widened.shape[2]
    pairs = rows // 2
    total = n_lat * pairs
    used = variables * rows
    lanes = given_t.shape[1]
    high = precondition(sigma_high)
    low = precondition(sigma_low)
    east = lax.rem(lon + 1, n_lon)
    west = lax.rem(lon + n_lon - 1, n_lon)
    final = n_lat - 1

    small = [
        pltpu.make_async_copy(source, landing, osem.at[k])
        for k, (source, landing) in enumerate(
            (
                (start_hbm.at[0], start),
                (prior_hbm, prior),
                (lift_w_hbm.at[0], lift_w),
                (gain_hbm, gain),
                (head_hbm.at[0], head),
                (expand_hbm.at[0], expand),
                (shrink_hbm.at[0], shrink),
            )
        )
    ]
    for copy in small:
        copy.start()

    barrier = pltpu.get_barrier_semaphore()

    def greet(device):
        pl.semaphore_signal(barrier, inc=1, device_id=device, device_id_type=MESH)

    for step in range(1, n_lat):
        greet((section, lax.rem(lat + step, n_lat), lon))
    for k in range(n_lat):
        greet((1 - section, k, lon))

    @pl.when(lat == 0)
    def _():
        for k in range(n_lat):
            greet((section, k, west))

    @pl.when(lat == final)
    def _():
        for k in range(n_lat):
            greet((section, k, east))

    copies = [
        pltpu.make_async_copy(
            conv0a.at[0], w0a.at[pl.ds(0, 3), :, :, pl.ds(0, c0)], wsem.at[0]
        ),
        pltpu.make_async_copy(
            conv0a.at[0], w0a.at[pl.ds(1, 3), :, :, pl.ds(c0, c0)], wsem.at[1]
        ),
        pltpu.make_async_copy(conv1a.at[0], w1a, wsem.at[2]),
        pltpu.make_async_copy(conv1b.at[0], w1b, wsem.at[3]),
        pltpu.make_async_copy(
            conv0b.at[0], w0b.at[pl.ds(0, 3), :, :, pl.ds(0, c0)], wsem.at[4]
        ),
        pltpu.make_async_copy(
            conv0b.at[0], w0b.at[pl.ds(1, 3), :, :, pl.ds(c0, c0)], wsem.at[5]
        ),
    ]
    for copy in copies:
        copy.start()
    for folded in (w0a, w0b):
        blank = jnp.zeros((3, c0, c0), bf16)
        folded[3, :, :, 0:c0] = blank
        folded[0, :, :, c0 : 2 * c0] = blank
    for padded in (lifted, widened, inner, merged):
        blank = jnp.zeros((3,) + padded.shape[2:], bf16)
        padded[:, 0] = blank
        padded[:, total + 1] = blank

    def pick(base, count, parity):
        i = lax.broadcasted_iota(jnp.int32, (count, cols), 0)
        j = lax.broadcasted_iota(jnp.int32, (count, cols), 1)
        return jnp.where(j == 2 * (base + i) + parity, 1.0, 0.0)

    picks = [pick(k * own - HALO, wide, parity) for k in range(n_lat) for parity in range(2)]
    rim_picks = [
        pick(base, 2 * HALO, parity) for base in (half - HALO, -HALO) for parity in range(2)
    ]
    order = jnp.concatenate(picks + rim_picks, axis=0).astype(bf16)

    def turned(x):
        flat = x.reshape(used, cols)
        if lanes > used:
            flat = jnp.concatenate([flat, jnp.zeros((lanes - used, cols), f32)], axis=0)
        return dot_nt(order, flat.astype(bf16))

    small[0].wait()
    small[1].wait()
    full = jnp.concatenate(
        [turned(start[...].astype(f32)), turned(prior[...].astype(f32))], axis=1
    ).astype(bf16)
    for k in range(n_lat):
        outbox[k] = full[2 * wide * k : 2 * wide * (k + 1)]
    for side in range(2):
        at = 2 * wide * n_lat + 4 * HALO * side
        rims_out[side] = full[at : at + 4 * HALO]

    pl.semaphore_wait(barrier, 2 * n_lat + 1)

    def rim(side, source):
        return pltpu.make_async_remote_copy(
            src_ref=rims_out.at[side],
            dst_ref=rims_in.at[side, source],
            send_sem=rim_s.at[side],
            recv_sem=rim_r.at[side, source],
            device_id=(section, 0, east) if side == 0 else (section, final, west),
            device_id_type=MESH,
        )

    def box(step, source):
        to = lax.rem(lat + step, n_lat)
        return pltpu.make_async_remote_copy(
            src_ref=outbox.at[to],
            dst_ref=inbox.at[source],
            send_sem=box_s.at[step - 1],
            recv_sem=box_r.at[step - 1],
            device_id=(section, to, lon),
            device_id_type=MESH,
        )

    for side in range(2):
        rim(side, lat).start()
    for step in range(1, n_lat):
        box(step, lat).start()
    inbox[lat] = outbox[lat]

    for copy in small[2:]:
        copy.wait()
    spread_w = jnp.broadcast_to(
        lift_w[...].astype(f32)[:, None, :], (2 * variables, rows, c0)
    ).reshape(2 * used, c0)
    row_of = lax.rem(lax.broadcasted_iota(jnp.int32, (lanes, c0), 0), rows)
    for part in range(2):
        piece = spread_w[part * used : (part + 1) * used]
        if lanes > used:
            piece = jnp.concatenate([piece, jnp.zeros((lanes - used, c0), f32)], axis=0)
        for r in range(rows):
            wlift[
                r // 2, part * lanes : (part + 1) * lanes, (r % 2) * c0 : (r % 2 + 1) * c0
            ] = jnp.where(row_of == r, piece, 0.0).astype(bf16)
    v_id = lax.broadcasted_iota(jnp.int32, (variables, lanes), 0)
    l_id = lax.broadcasted_iota(jnp.int32, (variables, lanes), 1)
    spreading = jnp.where((l_id >= v_id * rows) & (l_id < (v_id + 1) * rows), 1.0, 0.0).astype(bf16)
    spread_h = lax.dot_general(
        head[...], spreading, (((0,), (0,)), ((), ())), preferred_element_type=f32
    )
    lane_row = lax.rem(lax.broadcasted_iota(jnp.int32, (c0, lanes), 1), rows)
    for r in range(rows):
        whead[r * c0 : (r + 1) * c0, :] = jnp.where(lane_row == r, spread_h, 0.0).astype(bf16)
    expand_w = expand[...]
    shrink_w = jnp.concatenate([shrink[...], shrink[...]], axis=1)
    gains = jnp.concatenate([gain[...], gain[...]], axis=1)
    shift[...] = jnp.where(diffuse, high[3], 0.0).astype(f32) * gains

    for step in range(1, n_lat):
        box(step, lax.rem(lat + n_lat - step, n_lat)).wait_recv()

    @pl.when(lat == 0)
    def _():
        for k in range(n_lat):
            rim(0, k).wait_recv()

    @pl.when(lat == final)
    def _():
        for k in range(n_lat):
            rim(1, k).wait_recv()

    scale = jnp.where(diffuse, high[0] * sigma_high, 1.0).astype(f32)
    near = lax.broadcasted_iota(jnp.int32, (2 * HALO, lanes), 0) < HALO
    depth = 2 * HALO
    for k in range(n_lat):
        block = inbox[k].astype(f32)
        left = jnp.where(lat == 0, rims_in[0, k].astype(f32), 0.0)
        right = jnp.where(lat == final, rims_in[1, k].astype(f32), 0.0)
        whole = []
        for parity in range(2):
            part = block[parity * wide : (parity + 1) * wide]
            rim_rows = slice(parity * depth, (parity + 1) * depth)
            whole += [
                part[:depth] + left[rim_rows],
                part[depth : wide - depth],
                part[wide - depth :] + right[rim_rows],
            ]
        whole = jnp.concatenate(whole, axis=0)
        place = slice(2 * wide * k, 2 * wide * (k + 1))
        given_t[place] = whole[:, :lanes]
        cells[place, :lanes] = (scale * whole[:, :lanes]).astype(bf16)
        cells[place, lanes:] = whole[:, lanes:].astype(bf16)

    def keep_fine(buffer, index, value):
        even, odd = value[:wide], value[wide:]
        buffer[0, index] = jnp.concatenate([pltpu.roll(odd, 1, 0), even], axis=0).astype(bf16)
        buffer[1, index] = value.astype(bf16)
        buffer[2, index] = jnp.concatenate(
            [odd, pltpu.roll(even, wide - 1, 0)], axis=0
        ).astype(bf16)

    def keep_coarse(buffer, index, value):
        buffer[0, index] = pltpu.roll(value, 1, 0).astype(bf16)
        buffer[1, index] = value.astype(bf16)
        buffer[2, index] = pltpu.roll(value, slab - 1, 0).astype(bf16)

    def fine_window(buffer, index):
        pieces = []
        for at, lane in ((0, c0), (1, 0), (1, c0), (2, 0)):
            pieces += [buffer[b, index + at, :, lane : lane + c0] for b in range(3)]
        return jnp.concatenate(pieces, axis=1)

    def coarse_window(buffer, index):
        return jnp.concatenate(
            [buffer[b, index + a] for a in range(3) for b in range(3)], axis=1
        )

    def stacked(window, buffer, indices):
        return jnp.concatenate([window(buffer, index) for index in indices], axis=0)

    def groups(count):
        return [range(at, at + count) for at in range(0, total, count)]

    def network(loading):
        for p in range(pairs):
            value = silu(dot(cells[...], wlift[p]) + shift[...])
            for k in range(n_lat):
                keep_fine(
                    lifted, k * pairs + p + 1, value[2 * wide * k : 2 * wide * (k + 1)]
                )
        if loading:
            copies[0].wait()
            copies[1].wait()
        for group in groups(total):
            acc = dot(stacked(fine_window, lifted, group), w0a[...].reshape(12 * c0, 2 * c0))
            value = silu(acc).astype(bf16)
            pooled = []
            for k, index in enumerate(group):
                piece = value[2 * wide * k : 2 * wide * (k + 1)]
                first[index] = piece
                piece = piece.astype(f32)
                piece = piece[:wide] + piece[wide:]
                pooled.append((piece[:, :c0] + piece[:, c0:]) * 0.25)
                if slab > wide:
                    pooled.append(jnp.zeros((slab - wide, c0), f32))
            result = dot(jnp.concatenate(pooled, axis=0).astype(bf16), expand_w)
            for k, index in enumerate(group):
                keep_coarse(widened, index + 1, result[slab * k : slab * (k + 1)])
        if loading:
            copies[2].wait()
        for group in groups(total):
            acc = dot(
                stacked(coarse_window, widened, group),
                w1a[...].reshape(9 * w1a.shape[1], w1a.shape[2]),
            )
            value = silu(acc)
            for k, index in enumerate(group):
                keep_coarse(inner, index + 1, value[slab * k : slab * (k + 1)])
        if loading:
            copies[3].wait()
        for group in groups(total):
            acc = dot(
                stacked(coarse_window, inner, group),
                w1b[...].reshape(9 * w1b.shape[1], w1b.shape[2]),
            )
            skip = jnp.concatenate([widened[1, index + 1] for index in group], axis=0)
            projected = dot((silu(acc) + skip.astype(f32)).astype(bf16), shrink_w)
            for k, index in enumerate(group):
                piece = projected[slab * k : slab * k + wide]
                keep_fine(
                    merged,
                    index + 1,
                    jnp.concatenate([piece, piece], axis=0) + first[index].astype(f32),
                )
        if loading:
            copies[4].wait()
            copies[5].wait()
        for group in groups(total):
            acc = dot(stacked(fine_window, merged, group), w0b[...].reshape(12 * c0, 2 * c0))
            value = silu(acc).astype(bf16)
            for k, index in enumerate(group):
                last[index] = value[2 * wide * k : 2 * wide * (k + 1)]
        return dot(
            jnp.concatenate(
                [
                    jnp.concatenate([last[index] for index in group], axis=1)
                    for group in groups(pairs)
                ],
                axis=0,
            ),
            whead[...],
        )

    def swap(to, source):
        return pltpu.make_async_remote_copy(
            src_ref=finished.at[to],
            dst_ref=arrived.at[source],
            send_sem=swap_s.at[to],
            recv_sem=swap_r.at[source],
            device_id=(1 - section, to, lon),
            device_id_type=MESH,
        )

    def hand_over(value):
        value = value.astype(bf16)
        for k in range(n_lat):
            finished[k] = value[2 * wide * k : 2 * wide * (k + 1)]
        for k in range(n_lat):
            swap(k, lat).start()

    first_out = network(True)
    for side in range(2):
        rim(side, lat).wait_send()
    for step in range(1, n_lat):
        box(step, lat).wait_send()

    @pl.when(jnp.logical_not(diffuse))
    def _():
        hand_over(first_out)

    @pl.when(diffuse)
    def _():
        noisy = sigma_high * given_t[...]
        first_denoised = high[1] * noisy + high[2] * first_out
        fresh = noisy + (sigma_low - sigma_high) / sigma_high * (noisy - first_denoised)
        moved[...] = fresh
        second_input = low[0] * fresh

        def part(k, parity):
            at = 2 * wide * k + wide * parity
            return second_input[at : at + wide]

        order_of = [(k, parity) for k in range(n_lat) for parity in range(2)]
        edges_out[0] = jnp.concatenate(
            [part(*at)[wide - depth :] for at in order_of], axis=0
        ).astype(bf16)
        edges_out[1] = jnp.concatenate([part(*at)[:depth] for at in order_of], axis=0).astype(bf16)

        to_east = (
            section,
            lax.rem(lat + 1, n_lat),
            lax.rem(lon + jnp.where(lat == final, 1, 0), n_lon),
        )
        to_west = (
            section,
            lax.rem(lat + n_lat - 1, n_lat),
            lax.rem(lon + n_lon - jnp.where(lat == 0, 1, 0), n_lon),
        )
        edges = [
            pltpu.make_async_remote_copy(
                src_ref=edges_out.at[side],
                dst_ref=edges_in.at[side],
                send_sem=edge_s.at[side],
                recv_sem=edge_r.at[side],
                device_id=(to_east, to_west)[side],
                device_id_type=MESH,
            )
            for side in range(2)
        ]
        for edge in edges:
            edge.start()
        shift[...] = low[3] * gains
        for edge in edges:
            edge.wait_recv()
        left = edges_in[0].astype(f32)
        right = edges_in[1].astype(f32)
        whole = []
        for n, at in enumerate(order_of):
            piece = part(*at)
            rim_rows = slice(depth * n, depth * (n + 1))
            whole += [
                jnp.where(near, left[rim_rows], piece[:depth]),
                piece[depth : wide - depth],
                jnp.where(near, piece[wide - depth :], right[rim_rows]),
            ]
        cells[:, :lanes] = jnp.concatenate(whole, axis=0).astype(bf16)
        second_out = network(False)
        second_denoised = low[1] * moved[...] + low[2] * second_out
        hand_over(cells[:, lanes:].astype(f32) + second_denoised)
        for edge in edges:
            edge.wait_send()

    def unpick(base):
        i = lax.broadcasted_iota(jnp.int32, (wide, cols), 0)
        j = lax.broadcasted_iota(jnp.int32, (wide, cols), 1)
        middle = (i >= HALO) & (i < wide - HALO)
        return [
            jnp.where(middle & (j == 2 * (base + i) + parity), 1.0, 0.0) for parity in range(2)
        ]

    back = jnp.concatenate(
        [piece for k in range(n_lat) for piece in unpick(k * own - HALO)], axis=0
    ).astype(bf16)
    a = lax.broadcasted_iota(jnp.int32, (lanes, lanes), 0)
    b = lax.broadcasted_iota(jnp.int32, (lanes, lanes), 1)
    eye = jnp.where(a == b, 1.0, 0.0).astype(bf16)
    for k in range(n_lat):
        swap(k, k).wait_recv()
    gathered = arrived[...].reshape(n_lat * 2 * wide, lanes)
    result = dot(dot_nt(eye, gathered).astype(bf16), back)[:used]
    out[0] = result.reshape(variables, rows, cols).astype(bf16)
    for k in range(n_lat):
        swap(k, lat).wait_send()


def on_device(
    n_lat,
    n_lon,
    start,
    prior_mean,
    lift_w,
    noise_gain,
    conv0a,
    expand,
    conv1a,
    conv1b,
    shrink,
    conv0b,
    head,
):
    variables, rows, cols = prior_mean.shape
    c0, c1 = expand.shape[1:]
    pairs = rows // 2
    total = n_lat * pairs
    wide = cols // 2 // n_lat + 2 * HALO
    slab = -(-wide // 16) * 16
    used = variables * rows
    lanes = -(-used // 128) * 128
    depth = 4 * HALO
    assert 2 * c0 == c1 and wide % 8 == 0 and n_lat % 2 == 0 and rows % 2 == 0
    split = (1, 3, 3, c0, c0)
    head_t = jnp.swapaxes(head, 1, 2)
    scratch = [
        pltpu.VMEM(start.shape[1:], bf16),
        pltpu.VMEM(prior_mean.shape, bf16),
        pltpu.VMEM(lift_w.shape[1:], bf16),
        pltpu.VMEM(noise_gain.shape, f32),
        pltpu.VMEM(expand.shape[1:], bf16),
        pltpu.VMEM(shrink.shape[1:], bf16),
        pltpu.VMEM(head_t.shape[1:], bf16),
        pltpu.VMEM((4, 3, c0, 2 * c0), bf16),
        pltpu.VMEM((4, 3, c0, 2 * c0), bf16),
        pltpu.VMEM((9, c1, c1), bf16),
        pltpu.VMEM((9, c1, c1), bf16),
        pltpu.VMEM((pairs, 2 * lanes, 2 * c0), bf16),
        pltpu.VMEM((rows * c0, lanes), bf16),
        pltpu.VMEM((n_lat, 2 * wide, 2 * lanes), bf16),
        pltpu.VMEM((n_lat, 2 * wide, 2 * lanes), bf16),
        pltpu.VMEM((2, depth, 2 * lanes), bf16),
        pltpu.VMEM((2, n_lat, depth, 2 * lanes), bf16),
        pltpu.VMEM((2, n_lat * depth, lanes), bf16),
        pltpu.VMEM((2, n_lat * depth, lanes), bf16),
        pltpu.VMEM((n_lat * 2 * wide, lanes), f32),
        pltpu.VMEM((n_lat * 2 * wide, lanes), f32),
        pltpu.VMEM((1, 2 * c0), f32),
        pltpu.VMEM((n_lat * 2 * wide, 2 * lanes), bf16),
        pltpu.VMEM((3, total + 2, 2 * wide, 2 * c0), bf16),
        pltpu.VMEM((total, 2 * wide, 2 * c0), bf16),
        pltpu.VMEM((3, total + 2, slab, c1), bf16),
        pltpu.VMEM((3, total + 2, slab, c1), bf16),
        pltpu.VMEM((3, total + 2, 2 * wide, 2 * c0), bf16),
        pltpu.VMEM((total, 2 * wide, 2 * c0), bf16),
        pltpu.VMEM((n_lat, 2 * wide, lanes), bf16),
        pltpu.VMEM((n_lat, 2 * wide, lanes), bf16),
        pltpu.SemaphoreType.DMA((7,)),
        pltpu.SemaphoreType.DMA((6,)),
        pltpu.SemaphoreType.DMA((n_lat - 1,)),
        pltpu.SemaphoreType.DMA((n_lat - 1,)),
        pltpu.SemaphoreType.DMA((2,)),
        pltpu.SemaphoreType.DMA((2, n_lat)),
        pltpu.SemaphoreType.DMA((2,)),
        pltpu.SemaphoreType.DMA((2,)),
        pltpu.SemaphoreType.DMA((n_lat,)),
        pltpu.SemaphoreType.DMA((n_lat,)),
    ]
    return pl.pallas_call(
        functools.partial(kernel, n_lat, n_lon),
        out_shape=jax.ShapeDtypeStruct((1, variables, rows, cols), bf16),
        in_specs=[pl.BlockSpec(memory_space=pl.ANY)] * 11,
        out_specs=pl.BlockSpec(memory_space=pltpu.VMEM),
        scratch_shapes=scratch,
        compiler_params=pltpu.CompilerParams(
            collective_id=0, has_side_effects=True, vmem_limit_bytes=60 * 2**20
        ),
    )(
        start,
        prior_mean,
        lift_w,
        noise_gain,
        conv0a.reshape(split),
        expand,
        conv1a,
        conv1b,
        shrink,
        conv0b.reshape(split),
        head_t,
    )


def solution(mesh):
    placed = (
        P("section", None, "lat", "lon"),
        P(None, "lat", "lon"),
        P("section", None, None),
        P("section", None),
        P("section", None, None, None),
        P("section", None, None),
        P("section", None, None, None),
        P("section", None, None, None),
        P("section", None, None),
        P("section", None, None, None),
        P("section", None, None),
    )
    return jax.shard_map(
        functools.partial(on_device, mesh.shape["lat"], mesh.shape["lon"]),
        mesh=mesh,
        in_specs=placed,
        out_specs=P("section", None, "lat", "lon"),
        check_vma=False,
    )
```

```python
import functools
import math

import jax
import jax.numpy as jnp
from jax import lax
from jax.experimental import pallas as pl
from jax.experimental.pallas import tpu as pltpu
from jax.sharding import PartitionSpec as P

sigma_data = 0.5
sigma_high = 2.0
sigma_low = 0.5

MESH = pl.DeviceIdType.MESH
bf16 = jnp.bfloat16
f32 = jnp.float32

HALO = 4


def precondition(sigma):
    total = sigma * sigma + sigma_data * sigma_data
    return (
        1.0 / math.sqrt(total),
        sigma_data * sigma_data / total,
        sigma * sigma_data / math.sqrt(total),
        math.log(sigma) / 4.0,
    )


def silu(x):
    half = 0.5 * x
    return half + half * jnp.tanh(half)


def dot(a, b):
    return jnp.dot(a, b, preferred_element_type=f32)


def dot_nt(a, b):
    return lax.dot_general(a, b, (((1,), (1,)), ((), ())), preferred_element_type=f32)


def kernel(
    n_lat,
    n_lon,
    start_hbm,
    prior_hbm,
    lift_w_hbm,
    gain_hbm,
    conv0a,
    expand_hbm,
    conv1a,
    conv1b,
    shrink_hbm,
    conv0b,
    head_hbm,
    out,
    start,
    prior,
    lift_w,
    gain,
    expand,
    shrink,
    head,
    w0a,
    w0b,
    w1a,
    w1b,
    wlift,
    whead,
    outbox,
    inbox,
    rims_out,
    rims_in,
    edges_out,
    edges_in,
    given_t,
    moved,
    shift,
    cells,
    lifted,
    first,
    widened,
    inner,
    merged,
    last,
    finished,
    arrived,
    osem,
    wsem,
    box_s,
    box_r,
    rim_s,
    rim_r,
    edge_s,
    edge_r,
    swap_s,
    swap_r,
):
    section = lax.axis_index("section")
    lat = lax.axis_index("lat")
    lon = lax.axis_index("lon")
    diffuse = section == 1
    variables, rows, cols = prior.shape
    c0 = lift_w.shape[-1]
    half = cols // 2
    own = half // n_lat
    wide = own + 2 * HALO
    slab = widened.shape[2]
    pairs = rows // 2
    total = n_lat * pairs
    used = variables * rows
    lanes = given_t.shape[1]
    high = precondition(sigma_high)
    low = precondition(sigma_low)
    east = lax.rem(lon + 1, n_lon)
    west = lax.rem(lon + n_lon - 1, n_lon)
    final = n_lat - 1

    small = [
        pltpu.make_async_copy(source, landing, osem.at[k])
        for k, (source, landing) in enumerate(
            (
                (start_hbm.at[0], start),
                (prior_hbm, prior),
                (lift_w_hbm.at[0], lift_w),
                (gain_hbm, gain),
                (head_hbm.at[0], head),
                (expand_hbm.at[0], expand),
                (shrink_hbm.at[0], shrink),
            )
        )
    ]
    for copy in small:
        copy.start()

    barrier = pltpu.get_barrier_semaphore()

    def greet(device):
        pl.semaphore_signal(barrier, inc=1, device_id=device, device_id_type=MESH)

    for step in range(1, n_lat):
        greet((section, lax.rem(lat + step, n_lat), lon))
    for k in range(n_lat):
        greet((1 - section, k, lon))

    @pl.when(lat == 0)
    def _():
        for k in range(n_lat):
            greet((section, k, west))

    @pl.when(lat == final)
    def _():
        for k in range(n_lat):
            greet((section, k, east))

    copies = [
        pltpu.make_async_copy(
            conv0a.at[0], w0a.at[pl.ds(0, 3), :, :, pl.ds(0, c0)], wsem.at[0]
        ),
        pltpu.make_async_copy(
            conv0a.at[0], w0a.at[pl.ds(1, 3), :, :, pl.ds(c0, c0)], wsem.at[1]
        ),
        pltpu.make_async_copy(conv1a.at[0], w1a, wsem.at[2]),
        pltpu.make_async_copy(conv1b.at[0], w1b, wsem.at[3]),
        pltpu.make_async_copy(
            conv0b.at[0], w0b.at[pl.ds(0, 3), :, :, pl.ds(0, c0)], wsem.at[4]
        ),
        pltpu.make_async_copy(
            conv0b.at[0], w0b.at[pl.ds(1, 3), :, :, pl.ds(c0, c0)], wsem.at[5]
        ),
    ]
    for copy in copies:
        copy.start()
    for folded in (w0a, w0b):
        blank = jnp.zeros((3, c0, c0), bf16)
        folded[3, :, :, 0:c0] = blank
        folded[0, :, :, c0 : 2 * c0] = blank
    for padded in (lifted, widened, inner, merged):
        blank = jnp.zeros((3,) + padded.shape[2:], bf16)
        padded[:, 0] = blank
        padded[:, total + 1] = blank

    def pick(base, count, parity):
        i = lax.broadcasted_iota(jnp.int32, (count, cols), 0)
        j = lax.broadcasted_iota(jnp.int32, (count, cols), 1)
        return jnp.where(j == 2 * (base + i) + parity, 1.0, 0.0)

    picks = [pick(k * own - HALO, wide, parity) for k in range(n_lat) for parity in range(2)]
    rim_picks = [
        pick(base, 2 * HALO, parity) for base in (half - HALO, -HALO) for parity in range(2)
    ]
    order = jnp.concatenate(picks + rim_picks, axis=0).astype(bf16)

    def turned(x):
        flat = x.reshape(used, cols)
        if lanes > used:
            flat = jnp.concatenate([flat, jnp.zeros((lanes - used, cols), f32)], axis=0)
        return dot_nt(order, flat.astype(bf16))

    small[0].wait()
    small[1].wait()
    full = jnp.concatenate(
        [turned(start[...].astype(f32)), turned(prior[...].astype(f32))], axis=1
    ).astype(bf16)
    for k in range(n_lat):
        outbox[k] = full[2 * wide * k : 2 * wide * (k + 1)]
    for side in range(2):
        at = 2 * wide * n_lat + 4 * HALO * side
        rims_out[side] = full[at : at + 4 * HALO]

    pl.semaphore_wait(barrier, 2 * n_lat + 1)

    def rim(side, source):
        return pltpu.make_async_remote_copy(
            src_ref=rims_out.at[side],
            dst_ref=rims_in.at[side, source],
            send_sem=rim_s.at[side],
            recv_sem=rim_r.at[side, source],
            device_id=(section, 0, east) if side == 0 else (section, final, west),
            device_id_type=MESH,
        )

    def box(step, source):
        to = lax.rem(lat + step, n_lat)
        return pltpu.make_async_remote_copy(
            src_ref=outbox.at[to],
            dst_ref=inbox.at[source],
            send_sem=box_s.at[step - 1],
            recv_sem=box_r.at[step - 1],
            device_id=(section, to, lon),
            device_id_type=MESH,
        )

    for side in range(2):
        rim(side, lat).start()
    for step in range(1, n_lat):
        box(step, lat).start()
    inbox[lat] = outbox[lat]

    for copy in small[2:]:
        copy.wait()
    spread_w = jnp.broadcast_to(
        lift_w[...].astype(f32)[:, None, :], (2 * variables, rows, c0)
    ).reshape(2 * used, c0)
    row_of = lax.rem(lax.broadcasted_iota(jnp.int32, (lanes, c0), 0), rows)
    for part in range(2):
        piece = spread_w[part * used : (part + 1) * used]
        if lanes > used:
            piece = jnp.concatenate([piece, jnp.zeros((lanes - used, c0), f32)], axis=0)
        for r in range(rows):
            wlift[
                r // 2, part * lanes : (part + 1) * lanes, (r % 2) * c0 : (r % 2 + 1) * c0
            ] = jnp.where(row_of == r, piece, 0.0).astype(bf16)
    v_id = lax.broadcasted_iota(jnp.int32, (variables, lanes), 0)
    l_id = lax.broadcasted_iota(jnp.int32, (variables, lanes), 1)
    spreading = jnp.where((l_id >= v_id * rows) & (l_id < (v_id + 1) * rows), 1.0, 0.0).astype(bf16)
    spread_h = lax.dot_general(
        head[...], spreading, (((0,), (0,)), ((), ())), preferred_element_type=f32
    )
    lane_row = lax.rem(lax.broadcasted_iota(jnp.int32, (c0, lanes), 1), rows)
    for r in range(rows):
        whead[r * c0 : (r + 1) * c0, :] = jnp.where(lane_row == r, spread_h, 0.0).astype(bf16)
    expand_w = expand[...]
    shrink_w = jnp.concatenate([shrink[...], shrink[...]], axis=1)
    gains = jnp.concatenate([gain[...], gain[...]], axis=1)
    shift[...] = jnp.where(diffuse, high[3], 0.0).astype(f32) * gains

    for step in range(1, n_lat):
        box(step, lax.rem(lat + n_lat - step, n_lat)).wait_recv()

    @pl.when(lat == 0)
    def _():
        for k in range(n_lat):
            rim(0, k).wait_recv()

    @pl.when(lat == final)
    def _():
        for k in range(n_lat):
            rim(1, k).wait_recv()

    scale = jnp.where(diffuse, high[0] * sigma_high, 1.0).astype(f32)
    near = lax.broadcasted_iota(jnp.int32, (2 * HALO, lanes), 0) < HALO
    depth = 2 * HALO
    for k in range(n_lat):
        block = inbox[k].astype(f32)
        left = jnp.where(lat == 0, rims_in[0, k].astype(f32), 0.0)
        right = jnp.where(lat == final, rims_in[1, k].astype(f32), 0.0)
        whole = []
        for parity in range(2):
            part = block[parity * wide : (parity + 1) * wide]
            rim_rows = slice(parity * depth, (parity + 1) * depth)
            whole += [
                part[:depth] + left[rim_rows],
                part[depth : wide - depth],
                part[wide - depth :] + right[rim_rows],
            ]
        whole = jnp.concatenate(whole, axis=0)
        place = slice(2 * wide * k, 2 * wide * (k + 1))
        given_t[place] = whole[:, :lanes]
        cells[place, :lanes] = (scale * whole[:, :lanes]).astype(bf16)
        cells[place, lanes:] = whole[:, lanes:].astype(bf16)

    def keep_fine(buffer, index, value):
        even, odd = value[:wide], value[wide:]
        buffer[0, index] = jnp.concatenate([pltpu.roll(odd, 1, 0), even], axis=0).astype(bf16)
        buffer[1, index] = value.astype(bf16)
        buffer[2, index] = jnp.concatenate(
            [odd, pltpu.roll(even, wide - 1, 0)], axis=0
        ).astype(bf16)

    def keep_coarse(buffer, index, value):
        buffer[0, index] = pltpu.roll(value, 1, 0).astype(bf16)
        buffer[1, index] = value.astype(bf16)
        buffer[2, index] = pltpu.roll(value, slab - 1, 0).astype(bf16)

    def fine_window(buffer, index):
        pieces = []
        for at, lane in ((0, c0), (1, 0), (1, c0), (2, 0)):
            pieces += [buffer[b, index + at, :, lane : lane + c0] for b in range(3)]
        return jnp.concatenate(pieces, axis=1)

    def coarse_window(buffer, index):
        return jnp.concatenate(
            [buffer[b, index + a] for a in range(3) for b in range(3)], axis=1
        )

    def stacked(window, buffer, indices):
        return jnp.concatenate([window(buffer, index) for index in indices], axis=0)

    def groups(count):
        return [range(at, at + count) for at in range(0, total, count)]

    def network(loading):
        for p in range(pairs):
            value = silu(dot(cells[...], wlift[p]) + shift[...])
            for k in range(n_lat):
                keep_fine(
                    lifted, k * pairs + p + 1, value[2 * wide * k : 2 * wide * (k + 1)]
                )
        if loading:
            copies[0].wait()
            copies[1].wait()
        for group in groups(pairs // 2):
            acc = dot(stacked(fine_window, lifted, group), w0a[...].reshape(12 * c0, 2 * c0))
            value = silu(acc).astype(bf16)
            pooled = []
            for k, index in enumerate(group):
                piece = value[2 * wide * k : 2 * wide * (k + 1)]
                first[index] = piece
                piece = piece.astype(f32)
                piece = piece[:wide] + piece[wide:]
                pooled.append((piece[:, :c0] + piece[:, c0:]) * 0.25)
                if slab > wide:
                    pooled.append(jnp.zeros((slab - wide, c0), f32))
            result = dot(jnp.concatenate(pooled, axis=0).astype(bf16), expand_w)
            for k, index in enumerate(group):
                keep_coarse(widened, index + 1, result[slab * k : slab * (k + 1)])
        if loading:
            copies[2].wait()
        for group in groups(pairs):
            acc = dot(
                stacked(coarse_window, widened, group),
                w1a[...].reshape(9 * w1a.shape[1], w1a.shape[2]),
            )
            value = silu(acc)
            for k, index in enumerate(group):
                keep_coarse(inner, index + 1, value[slab * k : slab * (k + 1)])
        if loading:
            copies[3].wait()
        for group in groups(pairs):
            acc = dot(
                stacked(coarse_window, inner, group),
                w1b[...].reshape(9 * w1b.shape[1], w1b.shape[2]),
            )
            skip = jnp.concatenate([widened[1, index + 1] for index in group], axis=0)
            projected = dot((silu(acc) + skip.astype(f32)).astype(bf16), shrink_w)
            for k, index in enumerate(group):
                piece = projected[slab * k : slab * k + wide]
                keep_fine(
                    merged,
                    index + 1,
                    jnp.concatenate([piece, piece], axis=0) + first[index].astype(f32),
                )
        if loading:
            copies[4].wait()
            copies[5].wait()
        for group in groups(pairs // 2):
            acc = dot(stacked(fine_window, merged, group), w0b[...].reshape(12 * c0, 2 * c0))
            value = silu(acc).astype(bf16)
            for k, index in enumerate(group):
                last[index] = value[2 * wide * k : 2 * wide * (k + 1)]
        return dot(
            jnp.concatenate(
                [
                    jnp.concatenate([last[index] for index in group], axis=1)
                    for group in groups(pairs)
                ],
                axis=0,
            ),
            whead[...],
        )

    def swap(to, source):
        return pltpu.make_async_remote_copy(
            src_ref=finished.at[to],
            dst_ref=arrived.at[source],
            send_sem=swap_s.at[to],
            recv_sem=swap_r.at[source],
            device_id=(1 - section, to, lon),
            device_id_type=MESH,
        )

    def hand_over(value):
        value = value.astype(bf16)
        for k in range(n_lat):
            finished[k] = value[2 * wide * k : 2 * wide * (k + 1)]
        for k in range(n_lat):
            swap(k, lat).start()

    first_out = network(True)
    for side in range(2):
        rim(side, lat).wait_send()
    for step in range(1, n_lat):
        box(step, lat).wait_send()

    @pl.when(jnp.logical_not(diffuse))
    def _():
        hand_over(first_out)

    @pl.when(diffuse)
    def _():
        noisy = sigma_high * given_t[...]
        first_denoised = high[1] * noisy + high[2] * first_out
        fresh = noisy + (sigma_low - sigma_high) / sigma_high * (noisy - first_denoised)
        moved[...] = fresh
        second_input = low[0] * fresh

        def part(k, parity):
            at = 2 * wide * k + wide * parity
            return second_input[at : at + wide]

        order_of = [(k, parity) for k in range(n_lat) for parity in range(2)]
        edges_out[0] = jnp.concatenate(
            [part(*at)[wide - depth :] for at in order_of], axis=0
        ).astype(bf16)
        edges_out[1] = jnp.concatenate([part(*at)[:depth] for at in order_of], axis=0).astype(bf16)

        to_east = (
            section,
            lax.rem(lat + 1, n_lat),
            lax.rem(lon + jnp.where(lat == final, 1, 0), n_lon),
        )
        to_west = (
            section,
            lax.rem(lat + n_lat - 1, n_lat),
            lax.rem(lon + n_lon - jnp.where(lat == 0, 1, 0), n_lon),
        )
        edges = [
            pltpu.make_async_remote_copy(
                src_ref=edges_out.at[side],
                dst_ref=edges_in.at[side],
                send_sem=edge_s.at[side],
                recv_sem=edge_r.at[side],
                device_id=(to_east, to_west)[side],
                device_id_type=MESH,
            )
            for side in range(2)
        ]
        for edge in edges:
            edge.start()
        shift[...] = low[3] * gains
        for edge in edges:
            edge.wait_recv()
        left = edges_in[0].astype(f32)
        right = edges_in[1].astype(f32)
        whole = []
        for n, at in enumerate(order_of):
            piece = part(*at)
            rim_rows = slice(depth * n, depth * (n + 1))
            whole += [
                jnp.where(near, left[rim_rows], piece[:depth]),
                piece[depth : wide - depth],
                jnp.where(near, piece[wide - depth :], right[rim_rows]),
            ]
        cells[:, :lanes] = jnp.concatenate(whole, axis=0).astype(bf16)
        second_out = network(False)
        second_denoised = low[1] * moved[...] + low[2] * second_out
        hand_over(cells[:, lanes:].astype(f32) + second_denoised)
        for edge in edges:
            edge.wait_send()

    def unpick(base):
        i = lax.broadcasted_iota(jnp.int32, (wide, cols), 0)
        j = lax.broadcasted_iota(jnp.int32, (wide, cols), 1)
        middle = (i >= HALO) & (i < wide - HALO)
        return [
            jnp.where(middle & (j == 2 * (base + i) + parity), 1.0, 0.0) for parity in range(2)
        ]

    back = jnp.concatenate(
        [piece for k in range(n_lat) for piece in unpick(k * own - HALO)], axis=0
    ).astype(bf16)
    a = lax.broadcasted_iota(jnp.int32, (lanes, lanes), 0)
    b = lax.broadcasted_iota(jnp.int32, (lanes, lanes), 1)
    eye = jnp.where(a == b, 1.0, 0.0).astype(bf16)
    for k in range(n_lat):
        swap(k, k).wait_recv()
    gathered = arrived[...].reshape(n_lat * 2 * wide, lanes)
    result = dot(dot_nt(eye, gathered).astype(bf16), back)[:used]
    out[0] = result.reshape(variables, rows, cols).astype(bf16)
    for k in range(n_lat):
        swap(k, lat).wait_send()


def on_device(
    n_lat,
    n_lon,
    start,
    prior_mean,
    lift_w,
    noise_gain,
    conv0a,
    expand,
    conv1a,
    conv1b,
    shrink,
    conv0b,
    head,
):
    variables, rows, cols = prior_mean.shape
    c0, c1 = expand.shape[1:]
    pairs = rows // 2
    total = n_lat * pairs
    wide = cols // 2 // n_lat + 2 * HALO
    slab = -(-wide // 16) * 16
    used = variables * rows
    lanes = -(-used // 128) * 128
    depth = 4 * HALO
    assert 2 * c0 == c1 and wide % 8 == 0 and n_lat % 2 == 0 and rows % 2 == 0
    split = (1, 3, 3, c0, c0)
    head_t = jnp.swapaxes(head, 1, 2)
    scratch = [
        pltpu.VMEM(start.shape[1:], bf16),
        pltpu.VMEM(prior_mean.shape, bf16),
        pltpu.VMEM(lift_w.shape[1:], bf16),
        pltpu.VMEM(noise_gain.shape, f32),
        pltpu.VMEM(expand.shape[1:], bf16),
        pltpu.VMEM(shrink.shape[1:], bf16),
        pltpu.VMEM(head_t.shape[1:], bf16),
        pltpu.VMEM((4, 3, c0, 2 * c0), bf16),
        pltpu.VMEM((4, 3, c0, 2 * c0), bf16),
        pltpu.VMEM((9, c1, c1), bf16),
        pltpu.VMEM((9, c1, c1), bf16),
        pltpu.VMEM((pairs, 2 * lanes, 2 * c0), bf16),
        pltpu.VMEM((rows * c0, lanes), bf16),
        pltpu.VMEM((n_lat, 2 * wide, 2 * lanes), bf16),
        pltpu.VMEM((n_lat, 2 * wide, 2 * lanes), bf16),
        pltpu.VMEM((2, depth, 2 * lanes), bf16),
        pltpu.VMEM((2, n_lat, depth, 2 * lanes), bf16),
        pltpu.VMEM((2, n_lat * depth, lanes), bf16),
        pltpu.VMEM((2, n_lat * depth, lanes), bf16),
        pltpu.VMEM((n_lat * 2 * wide, lanes), f32),
        pltpu.VMEM((n_lat * 2 * wide, lanes), f32),
        pltpu.VMEM((1, 2 * c0), f32),
        pltpu.VMEM((n_lat * 2 * wide, 2 * lanes), bf16),
        pltpu.VMEM((3, total + 2, 2 * wide, 2 * c0), bf16),
        pltpu.VMEM((total, 2 * wide, 2 * c0), bf16),
        pltpu.VMEM((3, total + 2, slab, c1), bf16),
        pltpu.VMEM((3, total + 2, slab, c1), bf16),
        pltpu.VMEM((3, total + 2, 2 * wide, 2 * c0), bf16),
        pltpu.VMEM((total, 2 * wide, 2 * c0), bf16),
        pltpu.VMEM((n_lat, 2 * wide, lanes), bf16),
        pltpu.VMEM((n_lat, 2 * wide, lanes), bf16),
        pltpu.SemaphoreType.DMA((7,)),
        pltpu.SemaphoreType.DMA((6,)),
        pltpu.SemaphoreType.DMA((n_lat - 1,)),
        pltpu.SemaphoreType.DMA((n_lat - 1,)),
        pltpu.SemaphoreType.DMA((2,)),
        pltpu.SemaphoreType.DMA((2, n_lat)),
        pltpu.SemaphoreType.DMA((2,)),
        pltpu.SemaphoreType.DMA((2,)),
        pltpu.SemaphoreType.DMA((n_lat,)),
        pltpu.SemaphoreType.DMA((n_lat,)),
    ]
    return pl.pallas_call(
        functools.partial(kernel, n_lat, n_lon),
        out_shape=jax.ShapeDtypeStruct((1, variables, rows, cols), bf16),
        in_specs=[pl.BlockSpec(memory_space=pl.ANY)] * 11,
        out_specs=pl.BlockSpec(memory_space=pltpu.VMEM),
        scratch_shapes=scratch,
        compiler_params=pltpu.CompilerParams(
            collective_id=0, has_side_effects=True, vmem_limit_bytes=60 * 2**20
        ),
    )(
        start,
        prior_mean,
        lift_w,
        noise_gain,
        conv0a.reshape(split),
        expand,
        conv1a,
        conv1b,
        shrink,
        conv0b.reshape(split),
        head_t,
    )


def solution(mesh):
    placed = (
        P("section", None, "lat", "lon"),
        P(None, "lat", "lon"),
        P("section", None, None),
        P("section", None),
        P("section", None, None, None),
        P("section", None, None),
        P("section", None, None, None),
        P("section", None, None, None),
        P("section", None, None),
        P("section", None, None, None),
        P("section", None, None),
    )
    return jax.shard_map(
        functools.partial(on_device, mesh.shape["lat"], mesh.shape["lon"]),
        mesh=mesh,
        in_specs=placed,
        out_specs=P("section", None, "lat", "lon"),
        check_vma=False,
    )
```

```python
import functools
import math

import jax
import jax.numpy as jnp
from jax import lax
from jax.experimental import pallas as pl
from jax.experimental.pallas import tpu as pltpu
from jax.sharding import PartitionSpec as P

sigma_data = 0.5
sigma_high = 2.0
sigma_low = 0.5

MESH = pl.DeviceIdType.MESH
bf16 = jnp.bfloat16
f32 = jnp.float32

HALO = 4
RIM = 2 * HALO


def precondition(sigma):
    total = sigma * sigma + sigma_data * sigma_data
    return (
        1.0 / math.sqrt(total),
        sigma_data * sigma_data / total,
        sigma * sigma_data / math.sqrt(total),
        math.log(sigma) / 4.0,
    )


def silu(x):
    half = 0.5 * x
    return half + half * jnp.tanh(half)


def dot(a, b):
    return jnp.dot(a, b, preferred_element_type=f32)


def dot_nt(a, b):
    return lax.dot_general(a, b, (((1,), (1,)), ((), ())), preferred_element_type=f32)


def kernel(
    n_lat,
    n_lon,
    start_hbm,
    prior_hbm,
    lift_w_hbm,
    gain_hbm,
    conv0a,
    expand_hbm,
    conv1a,
    conv1b,
    shrink_hbm,
    conv0b,
    head_hbm,
    out,
    start,
    prior,
    lift_w,
    gain,
    expand,
    shrink,
    head,
    w0a,
    w0b,
    w1a,
    w1b,
    wlift,
    whead,
    outbox,
    inbox,
    rims_out,
    rims_in,
    given_t,
    prior_t,
    moved,
    shift,
    cells,
    lifted,
    first,
    widened,
    inner,
    merged,
    last,
    finished,
    arrived,
    osem,
    wsem,
    box_s,
    box_r,
    rim_s,
    rim_r,
    swap_s,
    swap_r,
):
    section = lax.axis_index("section")
    lat = lax.axis_index("lat")
    lon = lax.axis_index("lon")
    diffuse = section == 1
    variables, rows, cols = prior.shape
    c0 = lift_w.shape[-1]
    half = cols // 2
    own = half // n_lat
    broad = own + 2 * RIM
    slab = widened.shape[2]
    pairs = rows // 2
    total = n_lat * pairs
    used = variables * rows
    lanes = given_t.shape[1]
    high = precondition(sigma_high)
    low = precondition(sigma_low)
    east = lax.rem(lon + 1, n_lon)
    west = lax.rem(lon + n_lon - 1, n_lon)
    final = n_lat - 1

    small = [
        pltpu.make_async_copy(source, landing, osem.at[k])
        for k, (source, landing) in enumerate(
            (
                (start_hbm.at[0], start),
                (prior_hbm, prior),
                (lift_w_hbm.at[0], lift_w),
                (gain_hbm, gain),
                (head_hbm.at[0], head),
                (expand_hbm.at[0], expand),
                (shrink_hbm.at[0], shrink),
            )
        )
    ]
    for copy in small:
        copy.start()

    barrier = pltpu.get_barrier_semaphore()

    def greet(device):
        pl.semaphore_signal(barrier, inc=1, device_id=device, device_id_type=MESH)

    for step in range(1, n_lat):
        greet((section, lax.rem(lat + step, n_lat), lon))
    for k in range(n_lat):
        greet((1 - section, k, lon))

    @pl.when(lat == 0)
    def _():
        for k in range(n_lat):
            greet((section, k, west))

    @pl.when(lat == final)
    def _():
        for k in range(n_lat):
            greet((section, k, east))

    copies = [
        pltpu.make_async_copy(
            conv0a.at[0], w0a.at[pl.ds(0, 3), :, :, pl.ds(0, c0)], wsem.at[0]
        ),
        pltpu.make_async_copy(
            conv0a.at[0], w0a.at[pl.ds(1, 3), :, :, pl.ds(c0, c0)], wsem.at[1]
        ),
        pltpu.make_async_copy(conv1a.at[0], w1a, wsem.at[2]),
        pltpu.make_async_copy(conv1b.at[0], w1b, wsem.at[3]),
        pltpu.make_async_copy(
            conv0b.at[0], w0b.at[pl.ds(0, 3), :, :, pl.ds(0, c0)], wsem.at[4]
        ),
        pltpu.make_async_copy(
            conv0b.at[0], w0b.at[pl.ds(1, 3), :, :, pl.ds(c0, c0)], wsem.at[5]
        ),
    ]
    for copy in copies:
        copy.start()
    def pick(base, count, parity):
        i = lax.broadcasted_iota(jnp.int32, (count, cols), 0)
        j = lax.broadcasted_iota(jnp.int32, (count, cols), 1)
        return jnp.where(j == 2 * (base + i) + parity, 1.0, 0.0)

    picks = [pick(k * own - RIM, broad, parity) for k in range(n_lat) for parity in range(2)]
    rim_picks = [pick(base, RIM, parity) for base in (half - RIM, 0) for parity in range(2)]
    order = jnp.concatenate(picks + rim_picks, axis=0).astype(bf16)

    def turned(x):
        flat = x.reshape(used, cols)
        if lanes > used:
            flat = jnp.concatenate([flat, jnp.zeros((lanes - used, cols), f32)], axis=0)
        return dot_nt(order, flat.astype(bf16))

    small[0].wait()
    small[1].wait()
    full = jnp.concatenate(
        [turned(start[...].astype(f32)), turned(prior[...].astype(f32))], axis=1
    ).astype(bf16)
    for k in range(n_lat):
        outbox[k] = full[2 * broad * k : 2 * broad * (k + 1)]
    for side in range(2):
        at = 2 * broad * n_lat + 2 * RIM * side
        rims_out[side] = full[at : at + 2 * RIM]

    pl.semaphore_wait(barrier, 2 * n_lat + 1)

    def rim(side, source):
        return pltpu.make_async_remote_copy(
            src_ref=rims_out.at[side],
            dst_ref=rims_in.at[side, source],
            send_sem=rim_s.at[side],
            recv_sem=rim_r.at[side, source],
            device_id=(section, 0, east) if side == 0 else (section, final, west),
            device_id_type=MESH,
        )

    def box(step, source):
        to = lax.rem(lat + step, n_lat)
        return pltpu.make_async_remote_copy(
            src_ref=outbox.at[to],
            dst_ref=inbox.at[source],
            send_sem=box_s.at[step - 1],
            recv_sem=box_r.at[step - 1],
            device_id=(section, to, lon),
            device_id_type=MESH,
        )

    for side in range(2):
        rim(side, lat).start()
    for step in range(1, n_lat):
        box(step, lat).start()
    inbox[lat] = outbox[lat]

    for folded in (w0a, w0b):
        blank = jnp.zeros((3, c0, c0), bf16)
        folded[3, :, :, 0:c0] = blank
        folded[0, :, :, c0 : 2 * c0] = blank
    for padded in (lifted, widened, inner, merged):
        blank = jnp.zeros((3,) + padded.shape[2:], bf16)
        padded[:, 0] = blank
        padded[:, total + 1] = blank

    for copy in small[2:]:
        copy.wait()
    spread_w = jnp.broadcast_to(
        lift_w[...].astype(f32)[:, None, :], (2 * variables, rows, c0)
    ).reshape(2 * used, c0)
    row_of = lax.rem(lax.broadcasted_iota(jnp.int32, (lanes, c0), 0), rows)
    for part in range(2):
        piece = spread_w[part * used : (part + 1) * used]
        if lanes > used:
            piece = jnp.concatenate([piece, jnp.zeros((lanes - used, c0), f32)], axis=0)
        for r in range(rows):
            wlift[
                r // 2, part * lanes : (part + 1) * lanes, (r % 2) * c0 : (r % 2 + 1) * c0
            ] = jnp.where(row_of == r, piece, 0.0).astype(bf16)
    v_id = lax.broadcasted_iota(jnp.int32, (variables, lanes), 0)
    l_id = lax.broadcasted_iota(jnp.int32, (variables, lanes), 1)
    spreading = jnp.where((l_id >= v_id * rows) & (l_id < (v_id + 1) * rows), 1.0, 0.0).astype(bf16)
    spread_h = lax.dot_general(
        head[...], spreading, (((0,), (0,)), ((), ())), preferred_element_type=f32
    )
    lane_row = lax.rem(lax.broadcasted_iota(jnp.int32, (c0, lanes), 1), rows)
    for r in range(rows):
        whead[r * c0 : (r + 1) * c0, :] = jnp.where(lane_row == r, spread_h, 0.0).astype(bf16)
    expand_w = expand[...]
    shrink_w = jnp.concatenate([shrink[...], shrink[...]], axis=1)
    gains = jnp.concatenate([gain[...], gain[...]], axis=1)
    shift[...] = jnp.where(diffuse, high[3], 0.0).astype(f32) * gains

    for step in range(1, n_lat):
        box(step, lax.rem(lat + n_lat - step, n_lat)).wait_recv()

    @pl.when(lat == 0)
    def _():
        for k in range(n_lat):
            rim(0, k).wait_recv()

    @pl.when(lat == final)
    def _():
        for k in range(n_lat):
            rim(1, k).wait_recv()

    scale = jnp.where(diffuse, high[0] * sigma_high, 1.0).astype(f32)
    for k in range(n_lat):
        block = inbox[k].astype(f32)
        left = jnp.where(lat == 0, rims_in[0, k].astype(f32), 0.0)
        right = jnp.where(lat == final, rims_in[1, k].astype(f32), 0.0)
        whole = []
        for parity in range(2):
            part = block[parity * broad : (parity + 1) * broad]
            rim_rows = slice(parity * RIM, (parity + 1) * RIM)
            whole += [
                part[:RIM] + left[rim_rows],
                part[RIM : broad - RIM],
                part[broad - RIM :] + right[rim_rows],
            ]
        whole = jnp.concatenate(whole, axis=0)
        place = slice(2 * broad * k, 2 * broad * (k + 1))
        given_t[place] = whole[:, :lanes]
        prior_t[place] = whole[:, lanes:]
        cells[place, :lanes] = (scale * whole[:, :lanes]).astype(bf16)
        cells[place, lanes:] = whole[:, lanes:].astype(bf16)

    def keep_fine(buffer, index, value):
        wide = value.shape[0] // 2
        even, odd = value[:wide], value[wide:]
        place = slice(0, 2 * wide)
        buffer[0, index, place] = jnp.concatenate([pltpu.roll(odd, 1, 0), even], axis=0).astype(
            bf16
        )
        buffer[1, index, place] = value.astype(bf16)
        buffer[2, index, place] = jnp.concatenate(
            [odd, pltpu.roll(even, wide - 1, 0)], axis=0
        ).astype(bf16)

    def keep_coarse(buffer, index, value):
        buffer[0, index] = pltpu.roll(value, 1, 0).astype(bf16)
        buffer[1, index] = value.astype(bf16)
        buffer[2, index] = pltpu.roll(value, slab - 1, 0).astype(bf16)

    def fine_window(wide, buffer, index):
        pieces = []
        for at, lane in ((0, c0), (1, 0), (1, c0), (2, 0)):
            pieces += [buffer[b, index + at, 0 : 2 * wide, lane : lane + c0] for b in range(3)]
        return jnp.concatenate(pieces, axis=1)

    def coarse_window(buffer, index):
        return jnp.concatenate(
            [buffer[b, index + a] for a in range(3) for b in range(3)], axis=1
        )

    def stacked(window, buffer, indices):
        return jnp.concatenate([window(buffer, index) for index in indices], axis=0)

    def groups(count):
        return [range(at, at + count) for at in range(0, total, count)]

    def network(loading, wide):
        fine = functools.partial(fine_window, wide)
        tall = 2 * wide
        for p in range(pairs):
            value = silu(dot(cells[0 : n_lat * tall], wlift[p]) + shift[...])
            for k in range(n_lat):
                keep_fine(
                    lifted, k * pairs + p + 1, value[2 * wide * k : 2 * wide * (k + 1)]
                )
        if loading:
            copies[0].wait()
            copies[1].wait()
        for group in groups(pairs):
            acc = dot(stacked(fine, lifted, group), w0a[...].reshape(12 * c0, 2 * c0))
            value = silu(acc).astype(bf16)
            pooled = []
            for k, index in enumerate(group):
                piece = value[2 * wide * k : 2 * wide * (k + 1)]
                first[index, 0:tall] = piece
                piece = piece.astype(f32)
                piece = piece[:wide] + piece[wide:]
                pooled.append((piece[:, :c0] + piece[:, c0:]) * 0.25)
                if slab > wide:
                    pooled.append(jnp.zeros((slab - wide, c0), f32))
            result = dot(jnp.concatenate(pooled, axis=0).astype(bf16), expand_w)
            for k, index in enumerate(group):
                keep_coarse(widened, index + 1, result[slab * k : slab * (k + 1)])
        if loading:
            copies[2].wait()
        for group in groups(2 * pairs):
            acc = dot(
                stacked(coarse_window, widened, group),
                w1a[...].reshape(9 * w1a.shape[1], w1a.shape[2]),
            )
            value = silu(acc)
            for k, index in enumerate(group):
                keep_coarse(inner, index + 1, value[slab * k : slab * (k + 1)])
        if loading:
            copies[3].wait()
        for group in groups(2 * pairs):
            acc = dot(
                stacked(coarse_window, inner, group),
                w1b[...].reshape(9 * w1b.shape[1], w1b.shape[2]),
            )
            skip = jnp.concatenate([widened[1, index + 1] for index in group], axis=0)
            projected = dot((silu(acc) + skip.astype(f32)).astype(bf16), shrink_w)
            for k, index in enumerate(group):
                piece = projected[slab * k : slab * k + wide]
                keep_fine(
                    merged,
                    index + 1,
                    jnp.concatenate([piece, piece], axis=0) + first[index, 0:tall].astype(f32),
                )
        if loading:
            copies[4].wait()
            copies[5].wait()
        for group in groups(pairs):
            acc = dot(stacked(fine, merged, group), w0b[...].reshape(12 * c0, 2 * c0))
            value = silu(acc).astype(bf16)
            for k, index in enumerate(group):
                last[index, 0:tall] = value[2 * wide * k : 2 * wide * (k + 1)]
        return dot(
            jnp.concatenate(
                [
                    jnp.concatenate([last[index, 0:tall] for index in group], axis=1)
                    for group in groups(pairs)
                ],
                axis=0,
            ),
            whead[...],
        )

    def swap(to, source):
        return pltpu.make_async_remote_copy(
            src_ref=finished.at[to],
            dst_ref=arrived.at[source],
            send_sem=swap_s.at[to],
            recv_sem=swap_r.at[source],
            device_id=(1 - section, to, lon),
            device_id_type=MESH,
        )

    def hand_over(pieces):
        for k in range(n_lat):
            finished[k] = jnp.concatenate(pieces[2 * k : 2 * k + 2], axis=0).astype(bf16)
        for k in range(n_lat):
            swap(k, lat).start()

    def trimmed(ref, size, margin):
        return [
            ref[size * n + margin : size * (n + 1) - margin] for n in range(2 * n_lat)
        ]

    first_out = network(True, broad)
    for side in range(2):
        rim(side, lat).wait_send()
    for step in range(1, n_lat):
        box(step, lat).wait_send()

    @pl.when(jnp.logical_not(diffuse))
    def _():
        moved[...] = first_out
        hand_over(trimmed(moved, broad, RIM))

    @pl.when(diffuse)
    def _():
        noisy = sigma_high * given_t[...]
        first_denoised = high[1] * noisy + high[2] * first_out
        moved[...] = noisy + (sigma_low - sigma_high) / sigma_high * (noisy - first_denoised)
        wide = broad - 2 * HALO
        rows_in = slice(0, 2 * n_lat * wide)
        fresh = jnp.concatenate(trimmed(moved, broad, HALO), axis=0)
        near_prior = jnp.concatenate(trimmed(prior_t, broad, HALO), axis=0)
        cells[rows_in, :lanes] = (low[0] * fresh).astype(bf16)
        cells[rows_in, lanes:] = near_prior.astype(bf16)
        shift[...] = low[3] * gains
        second_out = network(False, wide)
        fresh = jnp.concatenate(trimmed(moved, broad, HALO), axis=0)
        second_denoised = low[1] * fresh + low[2] * second_out
        given_t[rows_in] = cells[rows_in, lanes:].astype(f32) + second_denoised
        hand_over(trimmed(given_t, wide, HALO))

    back = jnp.concatenate(
        [pick(k * own, own, parity) for k in range(n_lat) for parity in range(2)], axis=0
    ).astype(bf16)
    a = lax.broadcasted_iota(jnp.int32, (lanes, lanes), 0)
    b = lax.broadcasted_iota(jnp.int32, (lanes, lanes), 1)
    eye = jnp.where(a == b, 1.0, 0.0).astype(bf16)
    for k in range(n_lat):
        swap(k, k).wait_recv()
    gathered = arrived[...].reshape(cols, lanes)
    result = dot(dot_nt(eye, gathered).astype(bf16), back)[:used]
    out[0] = result.reshape(variables, rows, cols).astype(bf16)
    for k in range(n_lat):
        swap(k, lat).wait_send()


def on_device(
    n_lat,
    n_lon,
    start,
    prior_mean,
    lift_w,
    noise_gain,
    conv0a,
    expand,
    conv1a,
    conv1b,
    shrink,
    conv0b,
    head,
):
    variables, rows, cols = prior_mean.shape
    c0, c1 = expand.shape[1:]
    pairs = rows // 2
    total = n_lat * pairs
    own = cols // 2 // n_lat
    wide = own + 2 * RIM
    slab = -(-wide // 16) * 16
    used = variables * rows
    lanes = -(-used // 128) * 128
    depth = 2 * RIM
    assert 2 * c0 == c1 and wide % 8 == 0 and n_lat % 2 == 0 and rows % 2 == 0
    split = (1, 3, 3, c0, c0)
    head_t = jnp.swapaxes(head, 1, 2)
    scratch = [
        pltpu.VMEM(start.shape[1:], bf16),
        pltpu.VMEM(prior_mean.shape, bf16),
        pltpu.VMEM(lift_w.shape[1:], bf16),
        pltpu.VMEM(noise_gain.shape, f32),
        pltpu.VMEM(expand.shape[1:], bf16),
        pltpu.VMEM(shrink.shape[1:], bf16),
        pltpu.VMEM(head_t.shape[1:], bf16),
        pltpu.VMEM((4, 3, c0, 2 * c0), bf16),
        pltpu.VMEM((4, 3, c0, 2 * c0), bf16),
        pltpu.VMEM((9, c1, c1), bf16),
        pltpu.VMEM((9, c1, c1), bf16),
        pltpu.VMEM((pairs, 2 * lanes, 2 * c0), bf16),
        pltpu.VMEM((rows * c0, lanes), bf16),
        pltpu.VMEM((n_lat, 2 * wide, 2 * lanes), bf16),
        pltpu.VMEM((n_lat, 2 * wide, 2 * lanes), bf16),
        pltpu.VMEM((2, depth, 2 * lanes), bf16),
        pltpu.VMEM((2, n_lat, depth, 2 * lanes), bf16),
        pltpu.VMEM((n_lat * 2 * wide, lanes), f32),
        pltpu.VMEM((n_lat * 2 * wide, lanes), f32),
        pltpu.VMEM((n_lat * 2 * wide, lanes), f32),
        pltpu.VMEM((1, 2 * c0), f32),
        pltpu.VMEM((n_lat * 2 * wide, 2 * lanes), bf16),
        pltpu.VMEM((3, total + 2, 2 * wide, 2 * c0), bf16),
        pltpu.VMEM((total, 2 * wide, 2 * c0), bf16),
        pltpu.VMEM((3, total + 2, slab, c1), bf16),
        pltpu.VMEM((3, total + 2, slab, c1), bf16),
        pltpu.VMEM((3, total + 2, 2 * wide, 2 * c0), bf16),
        pltpu.VMEM((total, 2 * wide, 2 * c0), bf16),
        pltpu.VMEM((n_lat, 2 * own, lanes), bf16),
        pltpu.VMEM((n_lat, 2 * own, lanes), bf16),
        pltpu.SemaphoreType.DMA((7,)),
        pltpu.SemaphoreType.DMA((6,)),
        pltpu.SemaphoreType.DMA((n_lat - 1,)),
        pltpu.SemaphoreType.DMA((n_lat - 1,)),
        pltpu.SemaphoreType.DMA((2,)),
        pltpu.SemaphoreType.DMA((2, n_lat)),
        pltpu.SemaphoreType.DMA((n_lat,)),
        pltpu.SemaphoreType.DMA((n_lat,)),
    ]
    return pl.pallas_call(
        functools.partial(kernel, n_lat, n_lon),
        out_shape=jax.ShapeDtypeStruct((1, variables, rows, cols), bf16),
        in_specs=[pl.BlockSpec(memory_space=pl.ANY)] * 11,
        out_specs=pl.BlockSpec(memory_space=pltpu.VMEM),
        scratch_shapes=scratch,
        compiler_params=pltpu.CompilerParams(
            collective_id=0, has_side_effects=True, vmem_limit_bytes=60 * 2**20
        ),
    )(
        start,
        prior_mean,
        lift_w,
        noise_gain,
        conv0a.reshape(split),
        expand,
        conv1a,
        conv1b,
        shrink,
        conv0b.reshape(split),
        head_t,
    )


def solution(mesh):
    placed = (
        P("section", None, "lat", "lon"),
        P(None, "lat", "lon"),
        P("section", None, None),
        P("section", None),
        P("section", None, None, None),
        P("section", None, None),
        P("section", None, None, None),
        P("section", None, None, None),
        P("section", None, None),
        P("section", None, None, None),
        P("section", None, None),
    )
    return jax.shard_map(
        functools.partial(on_device, mesh.shape["lat"], mesh.shape["lon"]),
        mesh=mesh,
        in_specs=placed,
        out_specs=P("section", None, "lat", "lon"),
        check_vma=False,
    )
```

```python
import functools
import math

import jax
import jax.numpy as jnp
from jax import lax
from jax.experimental import pallas as pl
from jax.experimental.pallas import tpu as pltpu
from jax.sharding import PartitionSpec as P

sigma_data = 0.5
sigma_high = 2.0
sigma_low = 0.5

MESH = pl.DeviceIdType.MESH
bf16 = jnp.bfloat16
f32 = jnp.float32

HALO = 4
RIM = 2 * HALO


def precondition(sigma):
    total = sigma * sigma + sigma_data * sigma_data
    return (
        1.0 / math.sqrt(total),
        sigma_data * sigma_data / total,
        sigma * sigma_data / math.sqrt(total),
        math.log(sigma) / 4.0,
    )


def silu(x):
    half = 0.5 * x
    return half + half * jnp.tanh(half)


def dot(a, b):
    return jnp.dot(a, b, preferred_element_type=f32)


def dot_nt(a, b):
    return lax.dot_general(a, b, (((1,), (1,)), ((), ())), preferred_element_type=f32)


def kernel(
    n_lat,
    n_lon,
    start_hbm,
    prior_hbm,
    lift_w_hbm,
    gain_hbm,
    conv0a,
    expand_hbm,
    conv1a,
    conv1b,
    shrink_hbm,
    conv0b,
    head_hbm,
    out,
    start,
    prior,
    lift_w,
    gain,
    expand,
    shrink,
    head,
    w0a,
    w0b,
    w1a,
    w1b,
    wlift,
    whead,
    outbox,
    inbox,
    rims_out,
    rims_in,
    given_t,
    prior_t,
    moved,
    shift,
    cells,
    lifted,
    first,
    widened,
    inner,
    merged,
    last,
    finished,
    arrived,
    osem,
    wsem,
    box_s,
    box_r,
    rim_s,
    rim_r,
    swap_s,
    swap_r,
):
    section = lax.axis_index("section")
    lat = lax.axis_index("lat")
    lon = lax.axis_index("lon")
    diffuse = section == 1
    variables, rows, cols = prior.shape
    c0 = lift_w.shape[-1]
    half = cols // 2
    own = half // n_lat
    broad = own + 2 * RIM
    slab = widened.shape[2]
    pairs = rows // 2
    total = n_lat * pairs
    used = variables * rows
    lanes = given_t.shape[1]
    high = precondition(sigma_high)
    low = precondition(sigma_low)
    east = lax.rem(lon + 1, n_lon)
    west = lax.rem(lon + n_lon - 1, n_lon)
    final = n_lat - 1

    small = [
        pltpu.make_async_copy(source, landing, osem.at[k])
        for k, (source, landing) in enumerate(
            (
                (start_hbm.at[0], start),
                (prior_hbm, prior),
                (lift_w_hbm.at[0], lift_w),
                (gain_hbm, gain),
                (head_hbm.at[0], head),
                (expand_hbm.at[0], expand),
                (shrink_hbm.at[0], shrink),
            )
        )
    ]
    for copy in small:
        copy.start()

    barrier = pltpu.get_barrier_semaphore()

    def greet(device):
        pl.semaphore_signal(barrier, inc=1, device_id=device, device_id_type=MESH)

    for step in range(1, n_lat):
        greet((section, lax.rem(lat + step, n_lat), lon))
    for k in range(n_lat):
        greet((1 - section, k, lon))

    @pl.when(lat == 0)
    def _():
        for k in range(n_lat):
            greet((section, k, west))

    @pl.when(lat == final)
    def _():
        for k in range(n_lat):
            greet((section, k, east))

    copies = [
        pltpu.make_async_copy(
            conv0a.at[0], w0a.at[pl.ds(0, 3), :, :, pl.ds(0, c0)], wsem.at[0]
        ),
        pltpu.make_async_copy(
            conv0a.at[0], w0a.at[pl.ds(1, 3), :, :, pl.ds(c0, c0)], wsem.at[1]
        ),
        pltpu.make_async_copy(conv1a.at[0], w1a, wsem.at[2]),
        pltpu.make_async_copy(conv1b.at[0], w1b, wsem.at[3]),
        pltpu.make_async_copy(
            conv0b.at[0], w0b.at[pl.ds(0, 3), :, :, pl.ds(0, c0)], wsem.at[4]
        ),
        pltpu.make_async_copy(
            conv0b.at[0], w0b.at[pl.ds(1, 3), :, :, pl.ds(c0, c0)], wsem.at[5]
        ),
    ]
    for copy in copies:
        copy.start()
    def pick(base, count, parity):
        i = lax.broadcasted_iota(jnp.int32, (count, cols), 0)
        j = lax.broadcasted_iota(jnp.int32, (count, cols), 1)
        return jnp.where(j == 2 * (base + i) + parity, 1.0, 0.0)

    picks = [pick(k * own - RIM, broad, parity) for k in range(n_lat) for parity in range(2)]
    rim_picks = [pick(base, RIM, parity) for base in (half - RIM, 0) for parity in range(2)]
    order = jnp.concatenate(picks + rim_picks, axis=0).astype(bf16)

    def turned(x):
        flat = x.reshape(used, cols)
        if lanes > used:
            flat = jnp.concatenate([flat, jnp.zeros((lanes - used, cols), f32)], axis=0)
        return dot_nt(order, flat.astype(bf16))

    small[0].wait()
    small[1].wait()
    full = jnp.concatenate(
        [turned(start[...].astype(f32)), turned(prior[...].astype(f32))], axis=1
    ).astype(bf16)
    for k in range(n_lat):
        outbox[k] = full[2 * broad * k : 2 * broad * (k + 1)]
    for side in range(2):
        at = 2 * broad * n_lat + 2 * RIM * side
        rims_out[side] = full[at : at + 2 * RIM]

    pl.semaphore_wait(barrier, 2 * n_lat + 1)

    def rim(side, source):
        return pltpu.make_async_remote_copy(
            src_ref=rims_out.at[side],
            dst_ref=rims_in.at[side, source],
            send_sem=rim_s.at[side],
            recv_sem=rim_r.at[side, source],
            device_id=(section, 0, east) if side == 0 else (section, final, west),
            device_id_type=MESH,
        )

    def box(step, source):
        to = lax.rem(lat + step, n_lat)
        return pltpu.make_async_remote_copy(
            src_ref=outbox.at[to],
            dst_ref=inbox.at[source],
            send_sem=box_s.at[step - 1],
            recv_sem=box_r.at[step - 1],
            device_id=(section, to, lon),
            device_id_type=MESH,
        )

    for side in range(2):
        rim(side, lat).start()
    for step in range(1, n_lat):
        box(step, lat).start()
    inbox[lat] = outbox[lat]

    for folded in (w0a, w0b):
        blank = jnp.zeros((3, c0, c0), bf16)
        folded[3, :, :, 0:c0] = blank
        folded[0, :, :, c0 : 2 * c0] = blank
    for padded in (lifted, widened, inner, merged):
        blank = jnp.zeros((3,) + padded.shape[2:], bf16)
        padded[:, 0] = blank
        padded[:, total + 1] = blank

    for copy in small[2:]:
        copy.wait()
    spread_w = jnp.broadcast_to(
        lift_w[...].astype(f32)[:, None, :], (2 * variables, rows, c0)
    ).reshape(2 * used, c0)
    row_of = lax.rem(lax.broadcasted_iota(jnp.int32, (lanes, c0), 0), rows)
    for part in range(2):
        piece = spread_w[part * used : (part + 1) * used]
        if lanes > used:
            piece = jnp.concatenate([piece, jnp.zeros((lanes - used, c0), f32)], axis=0)
        for r in range(rows):
            wlift[
                r // 2, part * lanes : (part + 1) * lanes, (r % 2) * c0 : (r % 2 + 1) * c0
            ] = jnp.where(row_of == r, piece, 0.0).astype(bf16)
    v_id = lax.broadcasted_iota(jnp.int32, (variables, lanes), 0)
    l_id = lax.broadcasted_iota(jnp.int32, (variables, lanes), 1)
    spreading = jnp.where((l_id >= v_id * rows) & (l_id < (v_id + 1) * rows), 1.0, 0.0).astype(bf16)
    spread_h = lax.dot_general(
        head[...], spreading, (((0,), (0,)), ((), ())), preferred_element_type=f32
    )
    lane_row = lax.rem(lax.broadcasted_iota(jnp.int32, (c0, lanes), 1), rows)
    for r in range(rows):
        whead[r * c0 : (r + 1) * c0, :] = jnp.where(lane_row == r, spread_h, 0.0).astype(bf16)
    expand_w = expand[...]
    shrink_w = jnp.concatenate([shrink[...], shrink[...]], axis=1)
    gains = jnp.concatenate([gain[...], gain[...]], axis=1)
    shift[...] = jnp.where(diffuse, high[3], 0.0).astype(f32) * gains

    for step in range(1, n_lat):
        box(step, lax.rem(lat + n_lat - step, n_lat)).wait_recv()

    @pl.when(lat == 0)
    def _():
        for k in range(n_lat):
            rim(0, k).wait_recv()

    @pl.when(lat == final)
    def _():
        for k in range(n_lat):
            rim(1, k).wait_recv()

    scale = jnp.where(diffuse, high[0] * sigma_high, 1.0).astype(f32)
    for k in range(n_lat):
        block = inbox[k].astype(f32)
        left = jnp.where(lat == 0, rims_in[0, k].astype(f32), 0.0)
        right = jnp.where(lat == final, rims_in[1, k].astype(f32), 0.0)
        whole = []
        for parity in range(2):
            part = block[parity * broad : (parity + 1) * broad]
            rim_rows = slice(parity * RIM, (parity + 1) * RIM)
            whole += [
                part[:RIM] + left[rim_rows],
                part[RIM : broad - RIM],
                part[broad - RIM :] + right[rim_rows],
            ]
        whole = jnp.concatenate(whole, axis=0)
        place = slice(2 * broad * k, 2 * broad * (k + 1))
        given_t[place] = whole[:, :lanes]
        prior_t[place] = whole[:, lanes:]
        cells[place, :lanes] = (scale * whole[:, :lanes]).astype(bf16)
        cells[place, lanes:] = whole[:, lanes:].astype(bf16)

    def keep_fine(buffer, index, value):
        wide = value.shape[0] // 2
        even, odd = value[:wide], value[wide:]
        place = slice(0, 2 * wide)
        buffer[0, index, place] = jnp.concatenate([pltpu.roll(odd, 1, 0), even], axis=0).astype(
            bf16
        )
        buffer[1, index, place] = value.astype(bf16)
        buffer[2, index, place] = jnp.concatenate(
            [odd, pltpu.roll(even, wide - 1, 0)], axis=0
        ).astype(bf16)

    def keep_coarse(buffer, index, value):
        buffer[0, index] = pltpu.roll(value, 1, 0).astype(bf16)
        buffer[1, index] = value.astype(bf16)
        buffer[2, index] = pltpu.roll(value, slab - 1, 0).astype(bf16)

    def fine_window(wide, buffer, index):
        pieces = []
        for at, lane in ((0, c0), (1, 0), (1, c0), (2, 0)):
            pieces += [buffer[b, index + at, 0 : 2 * wide, lane : lane + c0] for b in range(3)]
        return jnp.concatenate(pieces, axis=1)

    def coarse_window(buffer, index):
        return jnp.concatenate(
            [buffer[b, index + a] for a in range(3) for b in range(3)], axis=1
        )

    def stacked(window, buffer, indices):
        return jnp.concatenate([window(buffer, index) for index in indices], axis=0)

    def groups(count):
        return [range(at, at + count) for at in range(0, total, count)]

    def network(loading, wide):
        fine = functools.partial(fine_window, wide)
        tall = 2 * wide
        for p in range(pairs):
            value = silu(dot(cells[0 : n_lat * tall], wlift[p]) + shift[...])
            for k in range(n_lat):
                keep_fine(
                    lifted, k * pairs + p + 1, value[2 * wide * k : 2 * wide * (k + 1)]
                )
        def loaded(*which):
            if loading:
                for n in which:
                    copies[n].wait()

        def down(group):
            return dot(stacked(fine, lifted, group), w0a[...].reshape(12 * c0, 2 * c0))

        def after_down(group, acc):
            value = silu(acc).astype(bf16)
            pooled = []
            for k, index in enumerate(group):
                piece = value[2 * wide * k : 2 * wide * (k + 1)]
                first[index, 0:tall] = piece
                piece = piece.astype(f32)
                piece = piece[:wide] + piece[wide:]
                pooled.append((piece[:, :c0] + piece[:, c0:]) * 0.25)
                if slab > wide:
                    pooled.append(jnp.zeros((slab - wide, c0), f32))
            result = dot(jnp.concatenate(pooled, axis=0).astype(bf16), expand_w)
            for k, index in enumerate(group):
                keep_coarse(widened, index + 1, result[slab * k : slab * (k + 1)])

        def coarse_a(group):
            return dot(
                stacked(coarse_window, widened, group),
                w1a[...].reshape(9 * w1a.shape[1], w1a.shape[2]),
            )

        def after_coarse_a(group, acc):
            value = silu(acc)
            for k, index in enumerate(group):
                keep_coarse(inner, index + 1, value[slab * k : slab * (k + 1)])

        def coarse_b(group):
            return dot(
                stacked(coarse_window, inner, group),
                w1b[...].reshape(9 * w1b.shape[1], w1b.shape[2]),
            )

        def after_coarse_b(group, acc):
            skip = jnp.concatenate([widened[1, index + 1] for index in group], axis=0)
            projected = dot((silu(acc) + skip.astype(f32)).astype(bf16), shrink_w)
            for k, index in enumerate(group):
                piece = projected[slab * k : slab * k + wide]
                keep_fine(
                    merged,
                    index + 1,
                    jnp.concatenate([piece, piece], axis=0) + first[index, 0:tall].astype(f32),
                )

        def up(group):
            return dot(stacked(fine, merged, group), w0b[...].reshape(12 * c0, 2 * c0))

        def after_up(group, acc):
            value = silu(acc).astype(bf16)
            for k, index in enumerate(group):
                last[index, 0:tall] = value[2 * wide * k : 2 * wide * (k + 1)]

        middle = total // 2
        tasks = [(down, after_down, group, (0, 1)) for group in groups(pairs)]
        tasks += [(coarse_a, after_coarse_a, group, (2,)) for group in groups(middle)]
        tasks += [
            (coarse_b, after_coarse_b, group, (3,))
            for group in (range(middle - 1), range(middle - 1, total))
        ]
        tasks += [(up, after_up, group, (4, 5)) for group in groups(pairs)]
        waited = set()
        pending = None
        for ahead, behind, group, weights in tasks:
            if weights not in waited:
                waited.add(weights)
                loaded(*weights)
            acc = ahead(group)
            if pending is not None:
                pending()
            pending = functools.partial(behind, group, acc)
        pending()
        return dot(
            jnp.concatenate(
                [
                    jnp.concatenate([last[index, 0:tall] for index in group], axis=1)
                    for group in groups(pairs)
                ],
                axis=0,
            ),
            whead[...],
        )

    def swap(to, source):
        return pltpu.make_async_remote_copy(
            src_ref=finished.at[to],
            dst_ref=arrived.at[source],
            send_sem=swap_s.at[to],
            recv_sem=swap_r.at[source],
            device_id=(1 - section, to, lon),
            device_id_type=MESH,
        )

    def hand_over(pieces):
        for k in range(n_lat):
            finished[k] = jnp.concatenate(pieces[2 * k : 2 * k + 2], axis=0).astype(bf16)
        for k in range(n_lat):
            swap(k, lat).start()

    def trimmed(ref, size, margin):
        return [
            ref[size * n + margin : size * (n + 1) - margin] for n in range(2 * n_lat)
        ]

    first_out = network(True, broad)
    for side in range(2):
        rim(side, lat).wait_send()
    for step in range(1, n_lat):
        box(step, lat).wait_send()

    @pl.when(jnp.logical_not(diffuse))
    def _():
        moved[...] = first_out
        hand_over(trimmed(moved, broad, RIM))

    @pl.when(diffuse)
    def _():
        noisy = sigma_high * given_t[...]
        first_denoised = high[1] * noisy + high[2] * first_out
        moved[...] = noisy + (sigma_low - sigma_high) / sigma_high * (noisy - first_denoised)
        wide = broad - 2 * HALO
        rows_in = slice(0, 2 * n_lat * wide)
        fresh = jnp.concatenate(trimmed(moved, broad, HALO), axis=0)
        near_prior = jnp.concatenate(trimmed(prior_t, broad, HALO), axis=0)
        cells[rows_in, :lanes] = (low[0] * fresh).astype(bf16)
        cells[rows_in, lanes:] = near_prior.astype(bf16)
        shift[...] = low[3] * gains
        second_out = network(False, wide)
        fresh = jnp.concatenate(trimmed(moved, broad, HALO), axis=0)
        second_denoised = low[1] * fresh + low[2] * second_out
        given_t[rows_in] = cells[rows_in, lanes:].astype(f32) + second_denoised
        hand_over(trimmed(given_t, wide, HALO))

    back = jnp.concatenate(
        [pick(k * own, own, parity) for k in range(n_lat) for parity in range(2)], axis=0
    ).astype(bf16)
    a = lax.broadcasted_iota(jnp.int32, (lanes, lanes), 0)
    b = lax.broadcasted_iota(jnp.int32, (lanes, lanes), 1)
    eye = jnp.where(a == b, 1.0, 0.0).astype(bf16)
    for k in range(n_lat):
        swap(k, k).wait_recv()
    gathered = arrived[...].reshape(cols, lanes)
    result = dot(dot_nt(eye, gathered).astype(bf16), back)[:used]
    out[0] = result.reshape(variables, rows, cols).astype(bf16)
    for k in range(n_lat):
        swap(k, lat).wait_send()


def on_device(
    n_lat,
    n_lon,
    start,
    prior_mean,
    lift_w,
    noise_gain,
    conv0a,
    expand,
    conv1a,
    conv1b,
    shrink,
    conv0b,
    head,
):
    variables, rows, cols = prior_mean.shape
    c0, c1 = expand.shape[1:]
    pairs = rows // 2
    total = n_lat * pairs
    own = cols // 2 // n_lat
    wide = own + 2 * RIM
    slab = -(-wide // 16) * 16
    used = variables * rows
    lanes = -(-used // 128) * 128
    depth = 2 * RIM
    assert total // 2 < total - pairs and pairs < total // 2 - 1
    assert 2 * c0 == c1 and wide % 8 == 0 and n_lat % 4 == 0 and rows % 4 == 0
    split = (1, 3, 3, c0, c0)
    head_t = jnp.swapaxes(head, 1, 2)
    scratch = [
        pltpu.VMEM(start.shape[1:], bf16),
        pltpu.VMEM(prior_mean.shape, bf16),
        pltpu.VMEM(lift_w.shape[1:], bf16),
        pltpu.VMEM(noise_gain.shape, f32),
        pltpu.VMEM(expand.shape[1:], bf16),
        pltpu.VMEM(shrink.shape[1:], bf16),
        pltpu.VMEM(head_t.shape[1:], bf16),
        pltpu.VMEM((4, 3, c0, 2 * c0), bf16),
        pltpu.VMEM((4, 3, c0, 2 * c0), bf16),
        pltpu.VMEM((9, c1, c1), bf16),
        pltpu.VMEM((9, c1, c1), bf16),
        pltpu.VMEM((pairs, 2 * lanes, 2 * c0), bf16),
        pltpu.VMEM((rows * c0, lanes), bf16),
        pltpu.VMEM((n_lat, 2 * wide, 2 * lanes), bf16),
        pltpu.VMEM((n_lat, 2 * wide, 2 * lanes), bf16),
        pltpu.VMEM((2, depth, 2 * lanes), bf16),
        pltpu.VMEM((2, n_lat, depth, 2 * lanes), bf16),
        pltpu.VMEM((n_lat * 2 * wide, lanes), f32),
        pltpu.VMEM((n_lat * 2 * wide, lanes), f32),
        pltpu.VMEM((n_lat * 2 * wide, lanes), f32),
        pltpu.VMEM((1, 2 * c0), f32),
        pltpu.VMEM((n_lat * 2 * wide, 2 * lanes), bf16),
        pltpu.VMEM((3, total + 2, 2 * wide, 2 * c0), bf16),
        pltpu.VMEM((total, 2 * wide, 2 * c0), bf16),
        pltpu.VMEM((3, total + 2, slab, c1), bf16),
        pltpu.VMEM((3, total + 2, slab, c1), bf16),
        pltpu.VMEM((3, total + 2, 2 * wide, 2 * c0), bf16),
        pltpu.VMEM((total, 2 * wide, 2 * c0), bf16),
        pltpu.VMEM((n_lat, 2 * own, lanes), bf16),
        pltpu.VMEM((n_lat, 2 * own, lanes), bf16),
        pltpu.SemaphoreType.DMA((7,)),
        pltpu.SemaphoreType.DMA((6,)),
        pltpu.SemaphoreType.DMA((n_lat - 1,)),
        pltpu.SemaphoreType.DMA((n_lat - 1,)),
        pltpu.SemaphoreType.DMA((2,)),
        pltpu.SemaphoreType.DMA((2, n_lat)),
        pltpu.SemaphoreType.DMA((n_lat,)),
        pltpu.SemaphoreType.DMA((n_lat,)),
    ]
    return pl.pallas_call(
        functools.partial(kernel, n_lat, n_lon),
        out_shape=jax.ShapeDtypeStruct((1, variables, rows, cols), bf16),
        in_specs=[pl.BlockSpec(memory_space=pl.ANY)] * 11,
        out_specs=pl.BlockSpec(memory_space=pltpu.VMEM),
        scratch_shapes=scratch,
        compiler_params=pltpu.CompilerParams(
            collective_id=0, has_side_effects=True, vmem_limit_bytes=60 * 2**20
        ),
    )(
        start,
        prior_mean,
        lift_w,
        noise_gain,
        conv0a.reshape(split),
        expand,
        conv1a,
        conv1b,
        shrink,
        conv0b.reshape(split),
        head_t,
    )


def solution(mesh):
    placed = (
        P("section", None, "lat", "lon"),
        P(None, "lat", "lon"),
        P("section", None, None),
        P("section", None),
        P("section", None, None, None),
        P("section", None, None),
        P("section", None, None, None),
        P("section", None, None, None),
        P("section", None, None),
        P("section", None, None, None),
        P("section", None, None),
    )
    return jax.shard_map(
        functools.partial(on_device, mesh.shape["lat"], mesh.shape["lon"]),
        mesh=mesh,
        in_specs=placed,
        out_specs=P("section", None, "lat", "lon"),
        check_vma=False,
    )
```
